32 devices in a mesh: mem: 16 (over z, y, x), camp: 2 (over core).
Axes of the slice: x: 2, y: 2, z: 4, core: 2. Of those that a mesh axis runs over, the one named last changes fastest.
Arguments:
- gains: bfloat16 [640, 128, 256], P('mem', None, 'camp'), may hold values from -14 to 14
- costs: bfloat16 [640, 128, 256], P('mem', None, 'camp'), may hold values from 0.5 to 2
- tile_rows: int32 [640, 2], P('mem', 'camp'), may hold values from 0 to 7, as said below
- tile_cols: int32 [640, 2], P('mem', 'camp'), may hold values from 0 to 1023
- tile_count: int32 [16, 2], P('mem', 'camp'), may hold values from 1 to 40, as said below
- duals: float32 [262144], P('camp'), may hold values from 0.005 to 0.04
- allowances: float32 [262144], P('camp'), may hold values from 0.02 to 0.16
Outputs:
- duals_out: float32 [262144], P('camp')
- usage_out: float32 [262144], P('camp')
- unused_share: float32 [16384], P('mem')
The draws below stay inside these ranges and needn't reach their ends.
Inputs may be any that keep to these rules, and one draw needn't show every extreme that they name: `tile_rows`: the live slots of one device name distinct pairs of member block and campaign block. `tile_count`: some device has all 40 slots live.
All inputs are finite; a program needn't handle non-finite values.
Results may differ from the reference program's by a relative error of at most 0.0003.
Values sent between devices are 32-bit elements; how exact they have to be, the bound alone decides.
A program may use at most 64 MiB of HBM per device.

```python
import math
import jax
import jax.numpy as jnp
from jax import lax

TILE = 128
MB = 8
CB = 1024
SLOTS = 40
ROUNDS = 3
SLOTS_ALL = 640
CAMP_COLS = 256
CAMPAIGNS = 262144
N_MEM = 16
N_CAMP = 2


def tile_pairs(key):
    key_list = jax.random.split(key, N_MEM * N_CAMP)
    chosen = jax.vmap(lambda single: jax.random.permutation(single, MB * CB)[:SLOTS])(key_list)
    chosen = chosen.reshape(N_MEM, N_CAMP, SLOTS).transpose(0, 2, 1).reshape(N_MEM * SLOTS, N_CAMP)
    return chosen.astype(jnp.int32)


def draw_tile_rows(key, part):
    paired = tile_pairs(key)
    return (paired // CB).astype(jnp.int32)


def draw_tile_cols(key, part):
    paired = tile_pairs(key)
    return (paired % CB).astype(jnp.int32)


def draw_tile_count(key, part):
    key = jax.random.fold_in(key, 7)
    key_one, key_two = jax.random.split(key)
    raw_draw = jax.random.randint(key_one, (N_MEM * N_CAMP,), 1, SLOTS + 1)
    slot_counts = jnp.maximum(1, raw_draw * raw_draw * raw_draw // (SLOTS * SLOTS))
    full_device = jax.random.randint(key_two, (), 0, N_MEM * N_CAMP)
    slot_counts = slot_counts.at[full_device].set(SLOTS)
    return slot_counts.reshape(N_MEM, N_CAMP).astype(jnp.int32)


def member_offsets(key, slot_blocks, lowest, highest):
    table = jax.random.uniform(key, (N_MEM, MB, TILE), jnp.float32, lowest, highest)
    device_ids = (jnp.arange(N_MEM * SLOTS) // SLOTS)[:, None]
    picked = table[device_ids, slot_blocks]
    picked = jnp.transpose(picked, (0, 2, 1))
    picked = jnp.broadcast_to(picked[:, :, :, None], (N_MEM * SLOTS, TILE, N_CAMP, TILE))
    return picked.reshape(N_MEM * SLOTS, TILE, N_CAMP * TILE)


def draw_gains(key, part):
    slot_blocks = tile_pairs(key) // CB
    key = jax.random.fold_in(key, 11)
    key_one = jax.random.fold_in(key, 0)
    key_six = jax.random.fold_in(key, 5)
    shape = (N_MEM * SLOTS, TILE, N_CAMP * TILE)
    drawn = jnp.clip(jax.random.normal(key_one, shape, jnp.float32), -6.0, 6.0)
    drawn = 0.05 * (drawn - member_offsets(key_six, slot_blocks, 2.0, 9.0))
    return drawn.astype(jnp.bfloat16)


def steps_of(stream_key, extent, pieces, least, largest):
    def one(position, parts):
        draws = jax.random.uniform(jax.random.fold_in(jax.random.fold_in(stream_key, 6), position), (parts,), jnp.float32, least / len(pieces), largest / len(pieces))
        return jnp.repeat(jnp.exp(draws), extent[position] // parts).reshape((-1,) + (1,) * (len(extent) - position - 1))

    factor_of = one(*pieces[0])
    for cut in pieces[1:]:
        factor_of = factor_of * one(*cut)
    return factor_of


def setup_inputs(seed: int = 0) -> dict:
    key_of = jax.random.split(jax.random.key(seed), 8)
    gains = draw_gains(jax.random.fold_in(key_of[7], 71), 0)
    costs = jnp.clip(jnp.exp(math.log(2.0) - 1.3862944 * jax.random.uniform(key_of[1], (SLOTS_ALL, TILE, CAMP_COLS), jnp.float32) ** steps_of(key_of[1], (SLOTS_ALL, TILE, CAMP_COLS), ((0, 16), (2, 2)), -0.2, 0.2)), 0.5, 2.0).astype(jnp.bfloat16)
    tile_rows = draw_tile_rows(jax.random.fold_in(key_of[7], 71), 0)
    tile_cols = draw_tile_cols(jax.random.fold_in(key_of[7], 71), 0)
    tile_count = draw_tile_count(jax.random.fold_in(key_of[7], 71), 0)
    duals = jnp.clip(jnp.exp(math.log(0.04) - 2.0794415 * jax.random.uniform(key_of[5], (CAMPAIGNS,), jnp.float32) ** steps_of(key_of[5], (CAMPAIGNS,), ((0, 2),), -0.2, 0.2)), 0.005, 0.04)
    allowances = jnp.clip(jnp.exp(math.log(0.16) - 2.0794415 * jax.random.uniform(key_of[6], (CAMPAIGNS,), jnp.float32) ** steps_of(key_of[6], (CAMPAIGNS,), ((0, 2),), -0.2, 0.2)), 0.02, 0.16)
    return dict(gains=gains, costs=costs, tile_rows=tile_rows, tile_cols=tile_cols, tile_count=tile_count, duals=duals, allowances=allowances)


SMOOTHING = 0.05
STEP_SIZE = 0.2


def member_rows(gain_t, cost_t, block_rows, block_cols, live_slot, price_blocks):
    group_ids = jnp.arange(N_CAMP)[None, :]
    price_tile = price_blocks[group_ids, block_cols]
    scores = (gain_t - cost_t * price_tile[:, None, :, :]) / SMOOTHING
    tile_top = jnp.max(scores, axis=3)
    onehot = (block_rows[None, :, :] == jnp.arange(MB)[:, None, None]) & live_slot[None, :, :]
    masked = jnp.where(onehot[:, :, None, :], tile_top[None], -jnp.inf)
    row_top = jnp.maximum(jnp.max(masked, axis=(1, 3)), 0.0)
    top_rows = jnp.transpose(row_top[block_rows], (0, 2, 1))
    exponent = jnp.exp(scores - top_rows[..., None])
    tile_sum = jnp.where(live_slot[:, None, :], jnp.sum(exponent, axis=3), 0.0)
    row_sum = jnp.einsum("bsg,srg->br", onehot.astype(jnp.float32), tile_sum, precision=lax.Precision.HIGHEST)
    denom = jnp.exp(-row_top) + row_sum
    alloc = exponent / jnp.transpose(denom[block_rows], (0, 2, 1))[..., None]
    column_use = jnp.where(live_slot[:, :, None], jnp.sum(cost_t * alloc, axis=1), 0.0)
    usage = jnp.zeros((N_CAMP, CB, TILE), jnp.float32).at[group_ids, block_cols].add(column_use)
    return usage, jnp.exp(-row_top) / denom


def reference(gains, costs, tile_rows, tile_cols, tile_count, duals, allowances):
    gain_all = gains.reshape(N_MEM, SLOTS, TILE, N_CAMP, TILE)
    cost_all = costs.reshape(N_MEM, SLOTS, TILE, N_CAMP, TILE)
    rows_all = tile_rows.reshape(N_MEM, SLOTS, N_CAMP)
    cols_all = tile_cols.reshape(N_MEM, SLOTS, N_CAMP)
    live_all = jnp.arange(SLOTS)[None, :, None] < tile_count[:, None, :]
    price = duals
    usage = jnp.zeros_like(duals)
    unused = jnp.zeros((N_MEM, MB, TILE), jnp.float32)
    for step in range(ROUNDS):
        price_blocks = price.reshape(N_CAMP, CB, TILE)

        def visit(running, index):
            used, spare = member_rows(gain_all[index].astype(jnp.float32), cost_all[index].astype(jnp.float32),
                                      rows_all[index], cols_all[index], live_all[index], price_blocks)
            return running + used, spare

        start = jnp.zeros((N_CAMP, CB, TILE), jnp.float32)
        summed, unused = lax.scan(visit, start, jnp.arange(N_MEM))
        usage = summed.reshape(-1)
        price = jnp.maximum(price + STEP_SIZE * (usage - allowances), 0.0)
    return price, usage, unused.reshape(-1)
```

```python
import functools
import math

import jax
import jax.numpy as jnp
from jax import lax
from jax.experimental import pallas as pl
from jax.experimental.pallas import tpu as pltpu
from jax.sharding import PartitionSpec as P

MB = 8
ROUNDS = 3
SMOOTHING = 0.05
STEP_SIZE = 0.2
SCALE = math.log2(math.e) / SMOOTHING
MESH = pl.DeviceIdType.MESH
UNROLL = 2


def near_first(extent):
    return sorted(range(1, extent), key=lambda d: (min(d, extent - d), d))


def kernel(
    n_mem, n_camp, plane,
    gains, costs, rows, cols, count, duals, allowances,
    price_out, usage_out, unused_out,
    g_raw, c_raw, gain, cost, score, run, exp_cost, top_of, weight_of,
    pair, ids, picked, onehot, parts, price, usage, allow, spare, prev, last,
    load_sem, z_send, z_recv, p_send, p_recv, c_send, c_recv,
):
    slots, tile = gain.shape[0], gain.shape[1]
    blocks = price.shape[0]
    me = lax.axis_index("mem")
    me_c = lax.axis_index("camp")
    deep = n_mem // plane
    z, b = lax.div(me, plane), lax.rem(me, plane)

    loads = [
        pltpu.make_async_copy(src, dst, load_sem.at[i])
        for i, (src, dst) in enumerate(
            ((gains, g_raw), (costs, c_raw), (duals, price), (allowances, allow))
        )
    ]
    for load in loads:
        load.start()

    def z_peer(d):
        return {"mem": lax.rem(z + d, deep) * plane + b, "camp": me_c}

    def p_peer(e):
        return {"mem": z * plane + lax.rem(b + e, plane), "camp": me_c}

    def c_peer(f):
        return {"mem": me, "camp": lax.rem(me_c + f, n_camp)}

    def owner(d, e):
        return lax.rem(z - d + deep, deep) * plane + lax.rem(b - e + plane, plane)

    barrier = pltpu.get_barrier_semaphore()
    peers = (
        [z_peer(d) for d in range(1, deep)]
        + [p_peer(e) for e in range(1, plane)]
        + [c_peer(f) for f in range(1, n_camp)]
    )
    for peer in peers:
        pl.semaphore_signal(barrier, inc=1, device_id=peer, device_id_type=MESH)

    def link(s, lasts):
        row = rows[s, 0]
        live = s < count[0, 0]
        before = jnp.int32(0)
        after = []
        for k in range(MB):
            mine = row == k
            before = jnp.where(mine, lasts[k], before)
            after.append(jnp.where(mine & live, s + 1, lasts[k]))
        prev[s] = before
        block = jnp.where(live, cols[s, 0], -1)
        ids[me, pl.ds(s, 1), :] = jnp.full((1, tile), block, jnp.int32)
        return tuple(after)

    lasts = lax.fori_loop(0, slots, link, (jnp.int32(0),) * MB)
    for k in range(MB):
        last[k] = lasts[k]
    run[0] = jnp.zeros((tile, tile), jnp.float32)

    pl.semaphore_wait(barrier, len(peers))

    def z_copy(buf, t, d):
        return pltpu.make_async_remote_copy(
            buf.at[me], buf.at[me], z_send.at[t, d], z_recv.at[t, d], z_peer(d), MESH
        )

    def p_copy(buf, t, d, e):
        block = buf.at[owner(d, 0)]
        return pltpu.make_async_remote_copy(
            block, block, p_send.at[t, d, e], p_recv.at[t, d, e], p_peer(e), MESH
        )

    def gather_start(buf, t):
        for d in near_first(deep):
            z_copy(buf, t, d).start()
        for e in near_first(plane):
            p_copy(buf, t, 0, e).start()

    def gather_relay(buf, t):
        for d in near_first(deep):
            block = buf.at[owner(d, 0)]
            pltpu.make_async_remote_copy(
                block, block, z_send.at[t, d], z_recv.at[t, d], z_peer(d), MESH
            ).wait_recv()
            for e in near_first(plane):
                p_copy(buf, t, d, e).start()

    def gather_wait(buf, t):
        for d in [0] + near_first(deep):
            for e in near_first(plane):
                block = buf.at[owner(d, e)]
                pltpu.make_async_remote_copy(
                    block, block, p_send.at[t, d, e], p_recv.at[t, d, e], p_peer(e), MESH
                ).wait_recv()

    def gather_drain(buf, t):
        for d in near_first(deep):
            z_copy(buf, t, d).wait_send()
        for d in range(deep):
            for e in near_first(plane):
                p_copy(buf, t, d, e).wait_send()

    gather_start(ids, 0)

    loads[0].wait()
    loads[1].wait()

    def widen(s, _):
        gain[s] = g_raw[s].astype(jnp.float32) * SCALE
        cost[s] = c_raw[s].astype(jnp.float32)
        return 0

    lax.fori_loop(0, slots, widen, 0, unroll=UNROLL)
    loads[2].wait()
    loads[3].wait()
    lane = lax.broadcasted_iota(jnp.int32, (tile, tile), 1)

    def camp_copy(t, f):
        return pltpu.make_async_remote_copy(
            pair.at[t, me_c], pair.at[t, me_c], c_send.at[t, f], c_recv.at[t, f], c_peer(f), MESH
        )

    for t in range(ROUNDS):
        def scores(s, _):
            row_price = price[pl.ds(cols[s, 0], 1), :] * SCALE
            now = gain[s] - cost[s] * row_price
            score[s] = now
            run[s + 1] = jnp.maximum(run[prev[s]], now)
            return 0

        lax.fori_loop(0, slots, scores, 0, unroll=UNROLL)

        def tops(k, packed):
            top = jnp.max(run[last[k]], axis=1, keepdims=True)
            top = jnp.broadcast_to(top, (tile, tile))
            top_of[k] = top
            return jnp.where(lane == k, top, packed)

        packed = lax.fori_loop(0, MB, tops, jnp.zeros((tile, tile), jnp.float32))

        def exponents(s, _):
            now = jnp.exp2(score[s] - top_of[rows[s, 0]])
            exp_cost[s] = now * cost[s]
            run[s + 1] = run[prev[s]] + now
            return 0

        lax.fori_loop(0, slots, exponents, 0, unroll=UNROLL)

        def sums(k, packed):
            total = jnp.sum(run[last[k]], axis=1, keepdims=True)
            return jnp.where(lane == k + MB, total, packed)

        pair[t, me_c] = lax.fori_loop(0, MB, sums, packed)
        for f in range(1, n_camp):
            camp_copy(t, f).start()

        if t == 0:
            gather_relay(ids, 0)
            gather_wait(ids, 0)
            flat = ids[...].reshape(n_mem * slots, tile).astype(jnp.float32)
            id_row = jnp.transpose(flat)[0:1, :]

            def mark(j, _):
                first = pl.multiple_of(j * tile, tile)
                here = lax.broadcasted_iota(jnp.int32, (tile, n_mem * slots), 0) + first
                onehot[pl.ds(first, tile), :] = jnp.where(
                    here.astype(jnp.float32) == id_row, 1.0, 0.0
                ).astype(jnp.bfloat16)
                return 0

            lax.fori_loop(0, blocks // tile, mark, 0)

        for f in range(1, n_camp):
            block = pair.at[t, lax.rem(me_c - f + n_camp, n_camp)]
            pltpu.make_async_remote_copy(
                block, block, c_send.at[t, f], c_recv.at[t, f], c_peer(f), MESH
            ).wait_recv()

        mine = pair[t, me_c]
        top = pair[t, 0]
        for c in range(1, n_camp):
            top = jnp.maximum(top, pair[t, c])
        denom = jnp.zeros((tile, tile), jnp.float32)
        for c in range(n_camp):
            theirs = pair[t, c]
            denom = denom + jnp.exp2(theirs - top) * pltpu.roll(theirs, tile - MB, 1)
        left = jnp.exp2(-top)
        denom = left + denom
        weight = jnp.exp2(mine - top) / denom
        if t == ROUNDS - 1:
            spare[...] = jnp.transpose(left / denom)[:MB]
        for k in range(MB):
            weight_of[k] = jnp.broadcast_to(weight[:, k : k + 1], (tile, tile))

        def uses(s, _):
            used = jnp.sum(exp_cost[s] * weight_of[rows[s, 0]], axis=0, keepdims=True)
            picked[t, me, pl.ds(s, 1), :] = used
            return 0

        lax.fori_loop(0, slots, uses, 0, unroll=UNROLL)
        place = lax.broadcasted_iota(jnp.int32, (slots, tile), 0)
        picked[t, me] = jnp.where(place < count[0, 0], picked[t, me], 0.0)

        gather_start(picked.at[t], t + 1)
        gather_relay(picked.at[t], t + 1)
        gather_wait(picked.at[t], t + 1)

        rest = picked[t].reshape(n_mem * slots, tile)
        for i in range(3):
            part = rest.astype(jnp.bfloat16)
            parts[:, i * tile : (i + 1) * tile] = part
            rest = rest - part.astype(jnp.float32)

        def update(j, _):
            here = pl.ds(pl.multiple_of(j * tile, tile), tile)
            summed = jnp.dot(onehot[here, :], parts[...], preferred_element_type=jnp.float32)
            now = summed[:, :tile] + summed[:, tile : 2 * tile] + summed[:, 2 * tile :]
            usage[here, :] = now
            price[here, :] = jnp.maximum(price[here, :] + STEP_SIZE * (now - allow[here, :]), 0.0)
            return 0

        lax.fori_loop(0, blocks // tile, update, 0)

    stores = [
        pltpu.make_async_copy(src, dst, load_sem.at[i])
        for i, (src, dst) in enumerate(
            ((price, price_out), (usage, usage_out), (spare, unused_out))
        )
    ]
    for store in stores:
        store.start()
    gather_drain(ids, 0)
    for t in range(ROUNDS):
        gather_drain(picked.at[t], t + 1)
        for f in range(1, n_camp):
            camp_copy(t, f).wait_send()
    for store in stores:
        store.wait()


def local(n_mem, n_camp, gains, costs, tile_rows, tile_cols, tile_count, duals, allowances):
    slots, tile, _ = gains.shape
    blocks = duals.shape[0] // tile
    plane = 4 if n_mem % 4 == 0 else 1
    deep = n_mem // plane
    f32, bf16 = jnp.float32, jnp.bfloat16
    anywhere = pl.BlockSpec(memory_space=pl.ANY)
    scalar = pl.BlockSpec(memory_space=pltpu.SMEM)
    dma = pltpu.SemaphoreType.DMA
    price, usage, unused = pl.pallas_call(
        functools.partial(kernel, n_mem, n_camp, plane),
        out_shape=(
            jax.ShapeDtypeStruct((blocks, tile), f32),
            jax.ShapeDtypeStruct((blocks, tile), f32),
            jax.ShapeDtypeStruct((MB, tile), f32),
        ),
        in_specs=[anywhere, anywhere, scalar, scalar, scalar, anywhere, anywhere],
        out_specs=(anywhere,) * 3,
        scratch_shapes=[
            pltpu.VMEM((slots, tile, tile), bf16),
            pltpu.VMEM((slots, tile, tile), bf16),
            pltpu.VMEM((slots, tile, tile), f32),
            pltpu.VMEM((slots, tile, tile), f32),
            pltpu.VMEM((slots, tile, tile), f32),
            pltpu.VMEM((slots + 1, tile, tile), f32),
            pltpu.VMEM((slots, tile, tile), f32),
            pltpu.VMEM((MB, tile, tile), f32),
            pltpu.VMEM((MB, tile, tile), f32),
            pltpu.VMEM((ROUNDS, n_camp, tile, tile), f32),
            pltpu.VMEM((n_mem, slots, tile), jnp.int32),
            pltpu.VMEM((ROUNDS, n_mem, slots, tile), f32),
            pltpu.VMEM((blocks, n_mem * slots), bf16),
            pltpu.VMEM((n_mem * slots, 3 * tile), bf16),
            pltpu.VMEM((blocks, tile), f32),
            pltpu.VMEM((blocks, tile), f32),
            pltpu.VMEM((blocks, tile), f32),
            pltpu.VMEM((MB, tile), f32),
            pltpu.SMEM((slots,), jnp.int32),
            pltpu.SMEM((MB,), jnp.int32),
            dma((4,)),
            dma((ROUNDS + 1, deep)),
            dma((ROUNDS + 1, deep)),
            dma((ROUNDS + 1, deep, plane)),
            dma((ROUNDS + 1, deep, plane)),
            dma((ROUNDS, n_camp)),
            dma((ROUNDS, n_camp)),
        ],
        compiler_params=pltpu.CompilerParams(
            collective_id=0, has_side_effects=True, vmem_limit_bytes=56 * 1024 * 1024
        ),
    )(
        gains, costs, tile_rows, tile_cols, tile_count,
        duals.reshape(blocks, tile), allowances.reshape(blocks, tile),
    )
    return price.reshape(-1), usage.reshape(-1), unused.reshape(-1)


def solution(mesh):
    return jax.shard_map(
        functools.partial(local, mesh.shape["mem"], mesh.shape["camp"]),
        mesh=mesh,
        in_specs=(
            P("mem", None, "camp"),
            P("mem", None, "camp"),
            P("mem", "camp"),
            P("mem", "camp"),
            P("mem", "camp"),
            P("camp"),
            P("camp"),
        ),
        out_specs=(P("camp"), P("camp"), P("mem")),
        check_vma=False,
    )
```

```python
import functools
import math

import jax
import jax.numpy as jnp
from jax import lax
from jax.experimental import pallas as pl
from jax.experimental.pallas import tpu as pltpu
from jax.sharding import PartitionSpec as P

MB = 8
ROUNDS = 3
SMOOTHING = 0.05
STEP_SIZE = 0.2
SCALE = math.log2(math.e) / SMOOTHING
MESH = pl.DeviceIdType.MESH
UNROLL = 8


def near_first(extent):
    return sorted(range(1, extent), key=lambda d: (min(d, extent - d), d))


def kernel(
    n_mem, n_camp, plane,
    gains, costs, rows, cols, count, duals, allowances,
    price, usage, spare,
    g_raw, c_raw, gain, cost, score, run, exp_cost, top_of, weight_of,
    pair, ids, picked, onehot, parts, allow, prev, last,
    load_sem, z_send, z_recv, p_send, p_recv, c_send, c_recv,
):
    slots, tile = gain.shape[0], gain.shape[1]
    blocks = price.shape[0]
    me = lax.axis_index("mem")
    me_c = lax.axis_index("camp")
    deep = n_mem // plane
    z, b = lax.div(me, plane), lax.rem(me, plane)

    loads = [
        pltpu.make_async_copy(src, dst, load_sem.at[i])
        for i, (src, dst) in enumerate(
            ((gains, g_raw), (costs, c_raw), (duals, price), (allowances, allow))
        )
    ]
    for load in loads:
        load.start()

    def z_peer(d):
        return {"mem": lax.rem(z + d, deep) * plane + b, "camp": me_c}

    def p_peer(e):
        return {"mem": z * plane + lax.rem(b + e, plane), "camp": me_c}

    def c_peer(f):
        return {"mem": me, "camp": lax.rem(me_c + f, n_camp)}

    def owner(d, e):
        return lax.rem(z - d + deep, deep) * plane + lax.rem(b - e + plane, plane)

    barrier = pltpu.get_barrier_semaphore()
    peers = (
        [z_peer(d) for d in range(1, deep)]
        + [p_peer(e) for e in range(1, plane)]
        + [c_peer(f) for f in range(1, n_camp)]
    )
    for peer in peers:
        pl.semaphore_signal(barrier, inc=1, device_id=peer, device_id_type=MESH)

    def link(s, lasts):
        row = rows[0, s]
        live = s < count[0, 0]
        before = jnp.int32(0)
        after = []
        for k in range(MB):
            mine = row == k
            before = jnp.where(mine, lasts[k], before)
            after.append(jnp.where(mine & live, s + 1, lasts[k]))
        prev[s] = before
        block = jnp.where(live, cols[0, s], -1)
        ids[me, pl.ds(s, 1), :] = jnp.full((1, tile), block, jnp.int32)
        return tuple(after)

    lasts = lax.fori_loop(0, slots, link, (jnp.int32(0),) * MB)
    for k in range(MB):
        last[k] = lasts[k]
    run[0] = jnp.zeros((tile, tile), jnp.float32)

    pl.semaphore_wait(barrier, len(peers))

    def z_copy(buf, t, d):
        return pltpu.make_async_remote_copy(
            buf.at[me], buf.at[me], z_send.at[t, d], z_recv.at[t, d], z_peer(d), MESH
        )

    def p_copy(buf, t, d, e):
        block = buf.at[owner(d, 0)]
        return pltpu.make_async_remote_copy(
            block, block, p_send.at[t, d, e], p_recv.at[t, d, e], p_peer(e), MESH
        )

    def gather_start(buf, t):
        for d in near_first(deep):
            z_copy(buf, t, d).start()
        for e in near_first(plane):
            p_copy(buf, t, 0, e).start()

    def gather_relay(buf, t):
        for d in near_first(deep):
            block = buf.at[owner(d, 0)]
            pltpu.make_async_remote_copy(
                block, block, z_send.at[t, d], z_recv.at[t, d], z_peer(d), MESH
            ).wait_recv()
            for e in near_first(plane):
                p_copy(buf, t, d, e).start()

    def gather_wait(buf, t):
        for d in [0] + near_first(deep):
            for e in near_first(plane):
                block = buf.at[owner(d, e)]
                pltpu.make_async_remote_copy(
                    block, block, p_send.at[t, d, e], p_recv.at[t, d, e], p_peer(e), MESH
                ).wait_recv()

    def gather_drain(buf, t):
        for d in near_first(deep):
            z_copy(buf, t, d).wait_send()
        for d in range(deep):
            for e in near_first(plane):
                p_copy(buf, t, d, e).wait_send()

    gather_start(ids, 0)

    loads[0].wait()
    loads[1].wait()

    loads[2].wait()
    loads[3].wait()
    lane = lax.broadcasted_iota(jnp.int32, (tile, tile), 1)

    def camp_copy(t, f):
        return pltpu.make_async_remote_copy(
            pair.at[t, me_c], pair.at[t, me_c], c_send.at[t, f], c_recv.at[t, f], c_peer(f), MESH
        )

    for t in range(ROUNDS):
        def scores(s, _):
            row_price = price[pl.ds(cols[0, s], 1), :] * SCALE
            if t == 0:
                worth = g_raw[s].astype(jnp.float32) * SCALE
                drawn = c_raw[s].astype(jnp.float32)
                gain[s] = worth
                cost[s] = drawn
            else:
                worth, drawn = gain[s], cost[s]
            now = worth - drawn * row_price
            score[s] = now
            run[s + 1] = jnp.maximum(run[prev[s]], now)
            return 0

        lax.fori_loop(0, slots, scores, 0, unroll=UNROLL)

        def tops(k, packed):
            top = jnp.max(run[last[k]], axis=1, keepdims=True)
            top = jnp.broadcast_to(top, (tile, tile))
            top_of[k] = top
            return jnp.where(lane == k, top, packed)

        packed = lax.fori_loop(0, MB, tops, jnp.zeros((tile, tile), jnp.float32), unroll=MB)

        def exponents(s, _):
            now = jnp.exp2(score[s] - top_of[rows[0, s]])
            exp_cost[s] = now * cost[s]
            run[s + 1] = run[prev[s]] + now
            return 0

        lax.fori_loop(0, slots, exponents, 0, unroll=UNROLL)

        def sums(k, packed):
            total = jnp.sum(run[last[k]], axis=1, keepdims=True)
            return jnp.where(lane == k + MB, total, packed)

        pair[t, me_c] = lax.fori_loop(0, MB, sums, packed, unroll=MB)
        for f in range(1, n_camp):
            camp_copy(t, f).start()

        if t == 0:
            gather_relay(ids, 0)
            gather_wait(ids, 0)
            flat = ids[...].reshape(n_mem * slots, tile).astype(jnp.float32)
            id_row = jnp.transpose(flat)[0:1, :]

            def mark(j, _):
                first = pl.multiple_of(j * tile, tile)
                here = lax.broadcasted_iota(jnp.int32, (tile, n_mem * slots), 0) + first
                onehot[pl.ds(first, tile), :] = jnp.where(
                    here.astype(jnp.float32) == id_row, 1.0, 0.0
                ).astype(jnp.bfloat16)
                return 0

            lax.fori_loop(0, blocks // tile, mark, 0)

        for f in range(1, n_camp):
            block = pair.at[t, lax.rem(me_c - f + n_camp, n_camp)]
            pltpu.make_async_remote_copy(
                block, block, c_send.at[t, f], c_recv.at[t, f], c_peer(f), MESH
            ).wait_recv()

        mine = pair[t, me_c]
        top = pair[t, 0]
        for c in range(1, n_camp):
            top = jnp.maximum(top, pair[t, c])
        denom = jnp.zeros((tile, tile), jnp.float32)
        for c in range(n_camp):
            theirs = pair[t, c]
            denom = denom + jnp.exp2(theirs - top) * pltpu.roll(theirs, tile - MB, 1)
        left = jnp.exp2(-top)
        denom = left + denom
        weight = jnp.exp2(mine - top) / denom
        if t == ROUNDS - 1:
            spare[...] = jnp.transpose(left / denom)[:MB]
        for k in range(MB):
            weight_of[k] = jnp.broadcast_to(weight[:, k : k + 1], (tile, tile))

        def uses(s, _):
            used = jnp.sum(exp_cost[s] * weight_of[rows[0, s]], axis=0, keepdims=True)
            picked[t, me, pl.ds(s, 1), :] = used
            return 0

        lax.fori_loop(0, slots, uses, 0, unroll=UNROLL)
        place = lax.broadcasted_iota(jnp.int32, (slots, tile), 0)
        picked[t, me] = jnp.where(place < count[0, 0], picked[t, me], 0.0)

        gather_start(picked.at[t], t + 1)
        gather_relay(picked.at[t], t + 1)
        gather_wait(picked.at[t], t + 1)

        rest = picked[t].reshape(n_mem * slots, tile)
        for i in range(3):
            part = rest.astype(jnp.bfloat16)
            parts[:, i * tile : (i + 1) * tile] = part
            rest = rest - part.astype(jnp.float32)

        summed = jnp.dot(onehot[...], parts[...], preferred_element_type=jnp.float32)
        now = summed[:, :tile] + summed[:, tile : 2 * tile] + summed[:, 2 * tile :]
        usage[...] = now
        price[...] = jnp.maximum(price[...] + STEP_SIZE * (now - allow[...]), 0.0)

    gather_drain(ids, 0)
    for t in range(ROUNDS):
        gather_drain(picked.at[t], t + 1)
        for f in range(1, n_camp):
            camp_copy(t, f).wait_send()


def hand_over(price, usage, spare, price_out, usage_out, unused_out, sem):
    stores = [
        pltpu.make_async_copy(src, dst, sem.at[i])
        for i, (src, dst) in enumerate(
            ((price, price_out), (usage, usage_out), (spare, unused_out))
        )
    ]
    for store in stores:
        store.start()
    for store in stores:
        store.wait()


def local(n_mem, n_camp, gains, costs, tile_rows, tile_cols, tile_count, duals, allowances):
    slots, tile, _ = gains.shape
    blocks = duals.shape[0] // tile
    plane = 4 if n_mem % 4 == 0 else 1
    deep = n_mem // plane
    f32, bf16 = jnp.float32, jnp.bfloat16
    anywhere = pl.BlockSpec(memory_space=pl.ANY)
    scalar = pl.BlockSpec(memory_space=pltpu.SMEM)
    dma = pltpu.SemaphoreType.DMA
    shapes = ((blocks, tile), (blocks, tile), (MB, tile))
    held = pl.pallas_call(
        functools.partial(kernel, n_mem, n_camp, plane),
        out_shape=tuple(pltpu.VMEM(shape, f32) for shape in shapes),
        in_specs=[anywhere, anywhere, scalar, scalar, scalar, anywhere, anywhere],
        out_specs=(pl.BlockSpec(memory_space=pltpu.VMEM),) * 3,
        scratch_shapes=[
            pltpu.VMEM((slots, tile, tile), bf16),
            pltpu.VMEM((slots, tile, tile), bf16),
            pltpu.VMEM((slots, tile, tile), f32),
            pltpu.VMEM((slots, tile, tile), f32),
            pltpu.VMEM((slots, tile, tile), f32),
            pltpu.VMEM((slots + 1, tile, tile), f32),
            pltpu.VMEM((slots, tile, tile), f32),
            pltpu.VMEM((MB, tile, tile), f32),
            pltpu.VMEM((MB, tile, tile), f32),
            pltpu.VMEM((ROUNDS, n_camp, tile, tile), f32),
            pltpu.VMEM((n_mem, slots, tile), jnp.int32),
            pltpu.VMEM((ROUNDS, n_mem, slots, tile), f32),
            pltpu.VMEM((blocks, n_mem * slots), bf16),
            pltpu.VMEM((n_mem * slots, 3 * tile), bf16),
            pltpu.VMEM((blocks, tile), f32),
            pltpu.SMEM((slots,), jnp.int32),
            pltpu.SMEM((MB,), jnp.int32),
            dma((4,)),
            dma((ROUNDS + 1, deep)),
            dma((ROUNDS + 1, deep)),
            dma((ROUNDS + 1, deep, plane)),
            dma((ROUNDS + 1, deep, plane)),
            dma((ROUNDS, n_camp)),
            dma((ROUNDS, n_camp)),
        ],
        compiler_params=pltpu.CompilerParams(
            collective_id=0, has_side_effects=True, vmem_limit_bytes=56 * 1024 * 1024
        ),
    )(
        gains, costs, tile_rows.T, tile_cols.T, tile_count,
        duals.reshape(blocks, tile), allowances.reshape(blocks, tile),
    )
    price, usage, unused = pl.pallas_call(
        hand_over,
        out_shape=tuple(jax.ShapeDtypeStruct(shape, f32) for shape in shapes),
        in_specs=[pl.BlockSpec(memory_space=pltpu.VMEM)] * 3,
        out_specs=(anywhere,) * 3,
        scratch_shapes=[dma((3,))],
    )(*held)
    return price.reshape(-1), usage.reshape(-1), unused.reshape(-1)


def solution(mesh):
    return jax.shard_map(
        functools.partial(local, mesh.shape["mem"], mesh.shape["camp"]),
        mesh=mesh,
        in_specs=(
            P("mem", None, "camp"),
            P("mem", None, "camp"),
            P("mem", "camp"),
            P("mem", "camp"),
            P("mem", "camp"),
            P("camp"),
            P("camp"),
        ),
        out_specs=(P("camp"), P("camp"), P("mem")),
        check_vma=False,
    )
```

```python
import functools
import math

import jax
import jax.numpy as jnp
from jax import lax
from jax.experimental import pallas as pl
from jax.experimental.pallas import tpu as pltpu
from jax.sharding import PartitionSpec as P

MB = 8
ROUNDS = 3
SMOOTHING = 0.05
STEP_SIZE = 0.2
SCALE = math.log2(math.e) / SMOOTHING
MESH = pl.DeviceIdType.MESH
UNROLL = 8


def flip(i, d):
    out, bit = i, 1
    while bit <= d:
        if d & bit:
            out = out + bit - 2 * bit * lax.rem(lax.div(i, bit), 2)
        bit *= 2
    return out


def kernel(
    n_mem, n_camp, plane,
    gains, costs, rows, cols, count, duals, allowances,
    price, usage, spare,
    g_raw, c_raw, gain, cost, score, run, exp_cost, top_of, weight_of,
    pair, ids, picked, onehot, own_hot, parts, allow,
    own_id, own_price, own_allow, prev, last,
    load_sem, z_send, z_recv, p_send, p_recv, c_send, c_recv,
):
    slots, tile = gain.shape[0], gain.shape[1]
    blocks = price.shape[0]
    me = lax.axis_index("mem")
    me_c = lax.axis_index("camp")
    deep = n_mem // plane
    z, b = lax.div(me, plane), lax.rem(me, plane)

    loads = [
        pltpu.make_async_copy(src, dst, load_sem.at[i])
        for i, (src, dst) in enumerate(
            ((gains, g_raw), (costs, c_raw), (duals, price), (allowances, allow))
        )
    ]
    for load in loads:
        load.start()

    def z_peer(d):
        return {"mem": flip(z, d) * plane + b, "camp": me_c}

    def p_peer(e):
        return {"mem": z * plane + flip(b, e), "camp": me_c}

    def c_peer(f):
        return {"mem": me, "camp": lax.rem(me_c + f, n_camp)}

    def owner(d, e):
        return flip(z, d) * plane + flip(b, e)

    barrier = pltpu.get_barrier_semaphore()
    peers = (
        [z_peer(d) for d in range(1, deep)]
        + [p_peer(e) for e in range(1, plane)]
        + [c_peer(f) for f in range(1, n_camp)]
    )
    for peer in peers:
        pl.semaphore_signal(barrier, inc=1, device_id=peer, device_id_type=MESH)

    id_rows = ids.shape[1]
    spot = lax.broadcasted_iota(jnp.int32, (id_rows, tile), 0) * tile
    spot = spot + lax.broadcasted_iota(jnp.int32, (id_rows, tile), 1) - me * slots

    def link(s, carry):
        lasts, packed = carry
        row = rows[0, s]
        live = s < count[0, 0]
        before = jnp.int32(0)
        after = []
        for k in range(MB):
            mine = row == k
            before = jnp.where(mine, lasts[k], before)
            after.append(jnp.where(mine & live, s + 1, lasts[k]))
        prev[s] = before
        block = jnp.where(live, cols[0, s] + 1, 0)
        own_id[pl.ds(s, 1), :] = jnp.full((1, tile), block, jnp.int32)
        return tuple(after), jnp.where(spot == s, block, packed)

    lasts, packed_ids = lax.fori_loop(
        0, slots, link, ((jnp.int32(0),) * MB, jnp.zeros((id_rows, tile), jnp.int32)), unroll=4
    )
    ids[me] = packed_ids
    for k in range(MB):
        last[k] = lasts[k]
    run[0] = jnp.zeros((tile, tile), jnp.float32)

    def z_copy(buf, t, d):
        return pltpu.make_async_remote_copy(
            buf.at[me], buf.at[me], z_send.at[t, d], z_recv.at[t, d], z_peer(d), MESH
        )

    def p_copy(buf, t, d, e):
        block = buf.at[owner(d, 0)]
        return pltpu.make_async_remote_copy(
            block, block, p_send.at[t, d, e], p_recv.at[t, d, e], p_peer(e), MESH
        )

    def gather_start(buf, t):
        for d in range(1, deep):
            z_copy(buf, t, d).start()
        for e in range(1, plane):
            p_copy(buf, t, 0, e).start()

    def gather_relay(buf, t):
        for d in range(1, deep):
            block = buf.at[owner(d, 0)]
            pltpu.make_async_remote_copy(
                block, block, z_send.at[t, d], z_recv.at[t, d], z_peer(d), MESH
            ).wait_recv()
            for e in range(1, plane):
                p_copy(buf, t, d, e).start()

    def gather_wait(buf, t):
        for d in range(deep):
            for e in range(1, plane):
                block = buf.at[owner(d, e)]
                pltpu.make_async_remote_copy(
                    block, block, p_send.at[t, d, e], p_recv.at[t, d, e], p_peer(e), MESH
                ).wait_recv()

    def gather_drain(buf, t):
        for d in range(1, deep):
            z_copy(buf, t, d).wait_send()
        for d in range(deep):
            for e in range(1, plane):
                p_copy(buf, t, d, e).wait_send()

    loads[2].wait()
    loads[3].wait()

    def fetch(s, _):
        here = pl.ds(cols[0, s], 1)
        own_price[pl.ds(s, 1), :] = price[here, :]
        own_allow[pl.ds(s, 1), :] = allow[here, :]
        return 0

    lax.fori_loop(0, slots, fetch, 0, unroll=UNROLL)
    loads[0].wait()
    loads[1].wait()
    lane = lax.broadcasted_iota(jnp.int32, (tile, tile), 1)

    def camp_copy(t, f):
        return pltpu.make_async_remote_copy(
            pair.at[t, me_c], pair.at[t, me_c], c_send.at[t, f], c_recv.at[t, f], c_peer(f), MESH
        )

    def mark():
        packed = ids[0]
        for p in range(1, n_mem):
            packed = packed + ids[p]
        for i in range(n_mem * slots // tile):
            id_row = packed[i : i + 1, :]
            own_hot[:, i * tile : (i + 1) * tile] = jnp.where(
                own_id[...] == id_row, 1.0, 0.0
            ).astype(jnp.bfloat16)
            for j in range(blocks // tile):
                here = lax.broadcasted_iota(jnp.int32, (tile, tile), 0) + (j * tile + 1)
                onehot[j * tile : (j + 1) * tile, i * tile : (i + 1) * tile] = jnp.where(
                    here == id_row, 1.0, 0.0
                ).astype(jnp.bfloat16)

    def summed_by(hot):
        three = jnp.dot(hot, parts[...], preferred_element_type=jnp.float32)
        return three[:, :tile] + three[:, tile : 2 * tile] + three[:, 2 * tile :]

    def advance(price, used, allow):
        return jnp.maximum(price + STEP_SIZE * (used - allow), 0.0)

    def dense():
        now = summed_by(onehot[...])
        usage[...] = now
        price[...] = advance(price[...], now, allow[...])

    for t in range(ROUNDS):
        def scores(s, _):
            row_price = own_price[pl.ds(s, 1), :] * SCALE
            if t == 0:
                worth = g_raw[s].astype(jnp.float32) * SCALE
                drawn = c_raw[s].astype(jnp.float32)
                gain[s] = worth
                cost[s] = drawn
            else:
                worth, drawn = gain[s], cost[s]
            now = worth - drawn * row_price
            score[s] = now
            run[s + 1] = jnp.maximum(run[prev[s]], now)
            return 0

        lax.fori_loop(0, slots, scores, 0, unroll=UNROLL)
        if t == 0:
            pl.semaphore_wait(barrier, len(peers))
            gather_start(ids, 0)

        def tops(k, packed):
            top = jnp.max(run[last[k]], axis=1, keepdims=True)
            top = jnp.broadcast_to(top, (tile, tile))
            top_of[k] = top
            return jnp.where(lane == k, top, packed)

        packed = lax.fori_loop(0, MB, tops, jnp.zeros((tile, tile), jnp.float32), unroll=MB)

        def exponents(s, _):
            now = jnp.exp2(score[s] - top_of[rows[0, s]])
            exp_cost[s] = now * cost[s]
            run[s + 1] = run[prev[s]] + now
            return 0

        lax.fori_loop(0, slots, exponents, 0, unroll=UNROLL)

        def sums(k, packed):
            total = jnp.sum(run[last[k]], axis=1, keepdims=True)
            return jnp.where(lane == k + MB, total, packed)

        pair[t, me_c] = lax.fori_loop(0, MB, sums, packed, unroll=MB)
        for f in range(1, n_camp):
            camp_copy(t, f).start()

        if t == 0:
            gather_relay(ids, 0)
        else:
            dense()

        for f in range(1, n_camp):
            block = pair.at[t, lax.rem(me_c - f + n_camp, n_camp)]
            pltpu.make_async_remote_copy(
                block, block, c_send.at[t, f], c_recv.at[t, f], c_peer(f), MESH
            ).wait_recv()

        mine = pair[t, me_c]
        top = pair[t, 0]
        for c in range(1, n_camp):
            top = jnp.maximum(top, pair[t, c])
        denom = jnp.zeros((tile, tile), jnp.float32)
        for c in range(n_camp):
            theirs = pair[t, c]
            denom = denom + jnp.exp2(theirs - top) * pltpu.roll(theirs, tile - MB, 1)
        left = jnp.exp2(-top)
        denom = left + denom
        weight = jnp.exp2(mine - top) / denom
        if t == ROUNDS - 1:
            spare[...] = jnp.transpose(left / denom)[:MB]
        for k in range(MB):
            weight_of[k] = jnp.broadcast_to(weight[:, k : k + 1], (tile, tile))

        def uses(s, _):
            used = jnp.sum(exp_cost[s] * weight_of[rows[0, s]], axis=0, keepdims=True)
            picked[t, me, pl.ds(s, 1), :] = used
            return 0

        lax.fori_loop(0, slots, uses, 0, unroll=UNROLL)
        place = lax.broadcasted_iota(jnp.int32, (slots, tile), 0)
        picked[t, me] = jnp.where(place < count[0, 0], picked[t, me], 0.0)

        gather_start(picked.at[t], t + 1)
        gather_relay(picked.at[t], t + 1)
        if t == 0:
            gather_wait(ids, 0)
            mark()
        gather_wait(picked.at[t], t + 1)

        rest = picked[t].reshape(n_mem * slots, tile)
        for i in range(3):
            part = rest.astype(jnp.bfloat16)
            parts[:, i * tile : (i + 1) * tile] = part
            rest = rest - part.astype(jnp.float32)

        if t < ROUNDS - 1:
            own_price[...] = advance(own_price[...], summed_by(own_hot[...]), own_allow[...])
        else:
            dense()

    gather_drain(ids, 0)
    for t in range(ROUNDS):
        gather_drain(picked.at[t], t + 1)
        for f in range(1, n_camp):
            camp_copy(t, f).wait_send()


def hand_over(price, usage, spare, price_out, usage_out, unused_out, sem):
    stores = [
        pltpu.make_async_copy(src, dst, sem.at[i])
        for i, (src, dst) in enumerate(
            ((price, price_out), (usage, usage_out), (spare, unused_out))
        )
    ]
    for store in stores:
        store.start()
    for store in stores:
        store.wait()


def local(n_mem, n_camp, gains, costs, tile_rows, tile_cols, tile_count, duals, allowances):
    slots, tile, _ = gains.shape
    blocks = duals.shape[0] // tile
    plane = 4 if n_mem % 4 == 0 else 1
    deep = n_mem // plane
    id_rows = -(-n_mem * slots // (8 * tile)) * 8
    f32, bf16 = jnp.float32, jnp.bfloat16
    anywhere = pl.BlockSpec(memory_space=pl.ANY)
    scalar = pl.BlockSpec(memory_space=pltpu.SMEM)
    dma = pltpu.SemaphoreType.DMA
    shapes = ((blocks, tile), (blocks, tile), (MB, tile))
    held = pl.pallas_call(
        functools.partial(kernel, n_mem, n_camp, plane),
        out_shape=tuple(pltpu.VMEM(shape, f32) for shape in shapes),
        in_specs=[anywhere, anywhere, scalar, scalar, scalar, anywhere, anywhere],
        out_specs=(pl.BlockSpec(memory_space=pltpu.VMEM),) * 3,
        scratch_shapes=[
            pltpu.VMEM((slots, tile, tile), bf16),
            pltpu.VMEM((slots, tile, tile), bf16),
            pltpu.VMEM((slots, tile, tile), f32),
            pltpu.VMEM((slots, tile, tile), f32),
            pltpu.VMEM((slots, tile, tile), f32),
            pltpu.VMEM((slots + 1, tile, tile), f32),
            pltpu.VMEM((slots, tile, tile), f32),
            pltpu.VMEM((MB, tile, tile), f32),
            pltpu.VMEM((MB, tile, tile), f32),
            pltpu.VMEM((ROUNDS, n_camp, tile, tile), f32),
            pltpu.VMEM((n_mem, id_rows, tile), jnp.int32),
            pltpu.VMEM((ROUNDS, n_mem, slots, tile), f32),
            pltpu.VMEM((blocks, n_mem * slots), bf16),
            pltpu.VMEM((slots, n_mem * slots), bf16),
            pltpu.VMEM((n_mem * slots, 3 * tile), bf16),
            pltpu.VMEM((blocks, tile), f32),
            pltpu.VMEM((slots, tile), jnp.int32),
            pltpu.VMEM((slots, tile), f32),
            pltpu.VMEM((slots, tile), f32),
            pltpu.SMEM((slots,), jnp.int32),
            pltpu.SMEM((MB,), jnp.int32),
            dma((4,)),
            dma((ROUNDS + 1, deep)),
            dma((ROUNDS + 1, deep)),
            dma((ROUNDS + 1, deep, plane)),
            dma((ROUNDS + 1, deep, plane)),
            dma((ROUNDS, n_camp)),
            dma((ROUNDS, n_camp)),
        ],
        compiler_params=pltpu.CompilerParams(
            collective_id=0, has_side_effects=True, vmem_limit_bytes=44 * 1024 * 1024
        ),
    )(
        gains, costs, tile_rows.T, tile_cols.T, tile_count,
        duals.reshape(blocks, tile), allowances.reshape(blocks, tile),
    )
    price, usage, unused = pl.pallas_call(
        hand_over,
        out_shape=tuple(jax.ShapeDtypeStruct(shape, f32) for shape in shapes),
        in_specs=[pl.BlockSpec(memory_space=pltpu.VMEM)] * 3,
        out_specs=(anywhere,) * 3,
        scratch_shapes=[dma((3,))],
        compiler_params=pltpu.CompilerParams(vmem_limit_bytes=1024 * 1024),
    )(*held)
    return price.reshape(-1), usage.reshape(-1), unused.reshape(-1)


def solution(mesh):
    return jax.shard_map(
        functools.partial(local, mesh.shape["mem"], mesh.shape["camp"]),
        mesh=mesh,
        in_specs=(
            P("mem", None, "camp"),
            P("mem", None, "camp"),
            P("mem", "camp"),
            P("mem", "camp"),
            P("mem", "camp"),
            P("camp"),
            P("camp"),
        ),
        out_specs=(P("camp"), P("camp"), P("mem")),
        check_vma=False,
    )
```

```python
import functools
import math

import jax
import jax.numpy as jnp
from jax import lax
from jax.experimental import pallas as pl
from jax.experimental.pallas import tpu as pltpu
from jax.sharding import PartitionSpec as P

MB = 8
ROUNDS = 3
SMOOTHING = 0.05
STEP_SIZE = 0.2
SCALE = math.log2(math.e) / SMOOTHING
MESH = pl.DeviceIdType.MESH
UNROLL = 8


def flip(i, d):
    out, bit = i, 1
    while bit <= d:
        if d & bit:
            out = out + bit - 2 * bit * lax.rem(lax.div(i, bit), 2)
        bit *= 2
    return out


def kernel(
    n_mem, n_camp, plane,
    gains, costs, rows_in, cols_in, count_in, duals, allowances,
    price, usage, spare,
    g_raw, c_raw, gain, cost, score, run, exp_cost, top_of, weight_of,
    pair, ids, picked, onehot, own_hot, parts, allow,
    own_id, own_price, own_allow, rows, cols, count, prev, last,
    load_sem, z_send, z_recv, p_send, p_recv, c_send, c_recv,
):
    slots, tile = gain.shape[0], gain.shape[1]
    blocks = price.shape[0]
    me = lax.axis_index("mem")
    me_c = lax.axis_index("camp")
    deep = n_mem // plane
    z, b = lax.div(me, plane), lax.rem(me, plane)

    loads = [
        pltpu.make_async_copy(src, dst, load_sem.at[i])
        for i, (src, dst) in enumerate(
            (
                (rows_in, rows), (cols_in, cols), (count_in, count),
                (duals, price), (allowances, allow), (gains, g_raw), (costs, c_raw),
            )
        )
    ]
    for load in loads:
        load.start()

    def z_peer(d):
        return {"mem": flip(z, d) * plane + b, "camp": me_c}

    def p_peer(e):
        return {"mem": z * plane + flip(b, e), "camp": me_c}

    def c_peer(f):
        return {"mem": me, "camp": lax.rem(me_c + f, n_camp)}

    def owner(d, e):
        return flip(z, d) * plane + flip(b, e)

    barrier = pltpu.get_barrier_semaphore()
    peers = (
        [z_peer(d) for d in range(1, deep)]
        + [p_peer(e) for e in range(1, plane)]
        + [c_peer(f) for f in range(1, n_camp)]
    )
    for peer in peers:
        pl.semaphore_signal(barrier, inc=1, device_id=peer, device_id_type=MESH)

    for load in loads[:3]:
        load.wait()
    id_rows = ids.shape[1]
    spot = lax.broadcasted_iota(jnp.int32, (id_rows, tile), 0) * tile
    spot = spot + lax.broadcasted_iota(jnp.int32, (id_rows, tile), 1) - me * slots

    def link(s, carry):
        lasts, packed = carry
        row = rows[0, s]
        live = s < count[0, 0]
        before = jnp.int32(0)
        after = []
        for k in range(MB):
            mine = row == k
            before = jnp.where(mine, lasts[k], before)
            after.append(jnp.where(mine & live, s + 1, lasts[k]))
        prev[s] = before
        block = jnp.where(live, cols[0, s] + 1, 0)
        own_id[pl.ds(s, 1), :] = jnp.full((1, tile), block, jnp.int32)
        return tuple(after), jnp.where(spot == s, block, packed)

    lasts, packed_ids = lax.fori_loop(
        0, slots, link, ((jnp.int32(0),) * MB, jnp.zeros((id_rows, tile), jnp.int32)), unroll=4
    )
    ids[me] = packed_ids
    for k in range(MB):
        last[k] = lasts[k]
    run[0] = jnp.zeros((tile, tile), jnp.float32)

    def z_copy(buf, t, d):
        return pltpu.make_async_remote_copy(
            buf.at[me], buf.at[me], z_send.at[t, d], z_recv.at[t, d], z_peer(d), MESH
        )

    def p_copy(buf, t, d, e):
        block = buf.at[owner(d, 0)]
        return pltpu.make_async_remote_copy(
            block, block, p_send.at[t, d, e], p_recv.at[t, d, e], p_peer(e), MESH
        )

    def gather_start(buf, t):
        for d in range(1, deep):
            z_copy(buf, t, d).start()
        for e in range(1, plane):
            p_copy(buf, t, 0, e).start()

    def gather_relay(buf, t):
        for d in range(1, deep):
            block = buf.at[owner(d, 0)]
            pltpu.make_async_remote_copy(
                block, block, z_send.at[t, d], z_recv.at[t, d], z_peer(d), MESH
            ).wait_recv()
            for e in range(1, plane):
                p_copy(buf, t, d, e).start()

    def gather_wait(buf, t, d):
        for e in range(1, plane):
            block = buf.at[owner(d, e)]
            pltpu.make_async_remote_copy(
                block, block, p_send.at[t, d, e], p_recv.at[t, d, e], p_peer(e), MESH
            ).wait_recv()

    def gather_drain(buf, t):
        for d in range(1, deep):
            z_copy(buf, t, d).wait_send()
        for d in range(deep):
            for e in range(1, plane):
                p_copy(buf, t, d, e).wait_send()

    loads[3].wait()
    loads[4].wait()

    def fetch(s, _):
        here = pl.ds(cols[0, s], 1)
        own_price[pl.ds(s, 1), :] = price[here, :]
        own_allow[pl.ds(s, 1), :] = allow[here, :]
        return 0

    lax.fori_loop(0, slots, fetch, 0, unroll=UNROLL)
    loads[5].wait()
    loads[6].wait()
    lane = lax.broadcasted_iota(jnp.int32, (tile, tile), 1)

    def camp_copy(t, f):
        return pltpu.make_async_remote_copy(
            pair.at[t, me_c], pair.at[t, me_c], c_send.at[t, f], c_recv.at[t, f], c_peer(f), MESH
        )

    def mark():
        packed = ids[0]
        for p in range(1, n_mem):
            packed = packed + ids[p]
        for i in range(n_mem * slots // tile):
            id_row = packed[i : i + 1, :]
            own_hot[:, i * tile : (i + 1) * tile] = jnp.where(
                own_id[...] == id_row, 1.0, 0.0
            ).astype(jnp.bfloat16)
            for j in range(blocks // tile):
                here = lax.broadcasted_iota(jnp.int32, (tile, tile), 0) + (j * tile + 1)
                onehot[j * tile : (j + 1) * tile, i * tile : (i + 1) * tile] = jnp.where(
                    here == id_row, 1.0, 0.0
                ).astype(jnp.bfloat16)

    def summed_by(hot):
        three = jnp.dot(hot, parts[...], preferred_element_type=jnp.float32)
        return three[:, :tile] + three[:, tile : 2 * tile] + three[:, 2 * tile :]

    def advance(price, used, allow):
        return jnp.maximum(price + STEP_SIZE * (used - allow), 0.0)

    def dense():
        now = summed_by(onehot[...])
        usage[...] = now
        price[...] = advance(price[...], now, allow[...])

    for t in range(ROUNDS):
        def scores(s, _):
            row_price = own_price[pl.ds(s, 1), :] * SCALE
            if t == 0:
                worth = g_raw[s].astype(jnp.float32) * SCALE
                drawn = c_raw[s].astype(jnp.float32)
                gain[s] = worth
                cost[s] = drawn
            else:
                worth, drawn = gain[s], cost[s]
            now = worth - drawn * row_price
            score[s] = now
            run[s + 1] = jnp.maximum(run[prev[s]], now)
            return 0

        lax.fori_loop(0, slots, scores, 0, unroll=UNROLL)
        if t == 0:
            pl.semaphore_wait(barrier, len(peers))
            gather_start(ids, 0)

        def tops(k, packed):
            top = jnp.max(run[last[k]], axis=1, keepdims=True)
            top = jnp.broadcast_to(top, (tile, tile))
            top_of[k] = top
            return jnp.where(lane == k, top, packed)

        packed = lax.fori_loop(0, MB, tops, jnp.zeros((tile, tile), jnp.float32), unroll=MB)

        def exponents(s, _):
            now = jnp.exp2(score[s] - top_of[rows[0, s]])
            exp_cost[s] = now * cost[s]
            run[s + 1] = run[prev[s]] + now
            return 0

        lax.fori_loop(0, slots, exponents, 0, unroll=UNROLL)

        def sums(k, packed):
            total = jnp.sum(run[last[k]], axis=1, keepdims=True)
            return jnp.where(lane == k + MB, total, packed)

        pair[t, me_c] = lax.fori_loop(0, MB, sums, packed, unroll=MB)
        for f in range(1, n_camp):
            camp_copy(t, f).start()

        if t == 0:
            gather_relay(ids, 0)
        else:
            dense()

        for f in range(1, n_camp):
            block = pair.at[t, lax.rem(me_c - f + n_camp, n_camp)]
            pltpu.make_async_remote_copy(
                block, block, c_send.at[t, f], c_recv.at[t, f], c_peer(f), MESH
            ).wait_recv()

        mine = pair[t, me_c]
        top = pair[t, 0]
        for c in range(1, n_camp):
            top = jnp.maximum(top, pair[t, c])
        denom = jnp.zeros((tile, tile), jnp.float32)
        for c in range(n_camp):
            theirs = pair[t, c]
            denom = denom + jnp.exp2(theirs - top) * pltpu.roll(theirs, tile - MB, 1)
        left = jnp.exp2(-top)
        denom = left + denom
        weight = jnp.exp2(mine - top) / denom
        if t == ROUNDS - 1:
            spare[...] = jnp.transpose(left / denom)[:MB]
        for k in range(MB):
            weight_of[k] = jnp.broadcast_to(weight[:, k : k + 1], (tile, tile))

        def uses(s, _):
            used = jnp.sum(exp_cost[s] * weight_of[rows[0, s]], axis=0, keepdims=True)
            picked[t, me, pl.ds(s, 1), :] = used
            return 0

        lax.fori_loop(0, slots, uses, 0, unroll=UNROLL)
        place = lax.broadcasted_iota(jnp.int32, (slots, tile), 0)
        picked[t, me] = jnp.where(place < count[0, 0], picked[t, me], 0.0)

        gather_start(picked.at[t], t + 1)
        gather_relay(picked.at[t], t + 1)
        if t == 0:
            for d in range(deep):
                gather_wait(ids, 0, d)
            mark()
        for d in range(deep):
            gather_wait(picked.at[t], t + 1, d)
            level = flip(z, d)
            rest = picked[t, pl.ds(level * plane, plane)].reshape(plane * slots, tile)
            here = pl.ds(pl.multiple_of(level * (plane * slots), 32), plane * slots)
            for i in range(3):
                part = rest.astype(jnp.bfloat16)
                parts[here, i * tile : (i + 1) * tile] = part
                rest = rest - part.astype(jnp.float32)

        if t < ROUNDS - 1:
            own_price[...] = advance(own_price[...], summed_by(own_hot[...]), own_allow[...])
        else:
            dense()

    gather_drain(ids, 0)
    for t in range(ROUNDS):
        gather_drain(picked.at[t], t + 1)
        for f in range(1, n_camp):
            camp_copy(t, f).wait_send()


def hand_over(price, usage, spare, price_out, usage_out, unused_out, sem):
    stores = [
        pltpu.make_async_copy(src, dst, sem.at[i])
        for i, (src, dst) in enumerate(
            ((price, price_out), (usage, usage_out), (spare, unused_out))
        )
    ]
    for store in stores:
        store.start()
    for store in stores:
        store.wait()


def local(n_mem, n_camp, gains, costs, tile_rows, tile_cols, tile_count, duals, allowances):
    slots, tile, _ = gains.shape
    blocks = duals.shape[0] // tile
    plane = 4 if n_mem % 4 == 0 else 1
    deep = n_mem // plane
    id_rows = -(-n_mem * slots // (8 * tile)) * 8
    f32, bf16 = jnp.float32, jnp.bfloat16
    anywhere = pl.BlockSpec(memory_space=pl.ANY)
    dma = pltpu.SemaphoreType.DMA
    shapes = ((blocks, tile), (blocks, tile), (MB, tile))
    held = pl.pallas_call(
        functools.partial(kernel, n_mem, n_camp, plane),
        out_shape=tuple(pltpu.VMEM(shape, f32) for shape in shapes),
        in_specs=[anywhere] * 7,
        out_specs=(pl.BlockSpec(memory_space=pltpu.VMEM),) * 3,
        scratch_shapes=[
            pltpu.VMEM((slots, tile, tile), bf16),
            pltpu.VMEM((slots, tile, tile), bf16),
            pltpu.VMEM((slots, tile, tile), f32),
            pltpu.VMEM((slots, tile, tile), f32),
            pltpu.VMEM((slots, tile, tile), f32),
            pltpu.VMEM((slots + 1, tile, tile), f32),
            pltpu.VMEM((slots, tile, tile), f32),
            pltpu.VMEM((MB, tile, tile), f32),
            pltpu.VMEM((MB, tile, tile), f32),
            pltpu.VMEM((ROUNDS, n_camp, tile, tile), f32),
            pltpu.VMEM((n_mem, id_rows, tile), jnp.int32),
            pltpu.VMEM((ROUNDS, n_mem, slots, tile), f32),
            pltpu.VMEM((blocks, n_mem * slots), bf16),
            pltpu.VMEM((slots, n_mem * slots), bf16),
            pltpu.VMEM((n_mem * slots, 3 * tile), bf16),
            pltpu.VMEM((blocks, tile), f32),
            pltpu.VMEM((slots, tile), jnp.int32),
            pltpu.VMEM((slots, tile), f32),
            pltpu.VMEM((slots, tile), f32),
            pltpu.SMEM((1, slots), jnp.int32),
            pltpu.SMEM((1, slots), jnp.int32),
            pltpu.SMEM((1, 1), jnp.int32),
            pltpu.SMEM((slots,), jnp.int32),
            pltpu.SMEM((MB,), jnp.int32),
            dma((7,)),
            dma((ROUNDS + 1, deep)),
            dma((ROUNDS + 1, deep)),
            dma((ROUNDS + 1, deep, plane)),
            dma((ROUNDS + 1, deep, plane)),
            dma((ROUNDS, n_camp)),
            dma((ROUNDS, n_camp)),
        ],
        compiler_params=pltpu.CompilerParams(
            collective_id=0, has_side_effects=True, vmem_limit_bytes=56 * 1024 * 1024
        ),
    )(
        gains, costs, tile_rows.T, tile_cols.T, tile_count,
        duals.reshape(blocks, tile), allowances.reshape(blocks, tile),
    )
    price, usage, unused = pl.pallas_call(
        hand_over,
        out_shape=tuple(jax.ShapeDtypeStruct(shape, f32) for shape in shapes),
        in_specs=[pl.BlockSpec(memory_space=pltpu.VMEM)] * 3,
        out_specs=(anywhere,) * 3,
        scratch_shapes=[dma((3,))],
        compiler_params=pltpu.CompilerParams(vmem_limit_bytes=1024 * 1024),
    )(*held)
    return price.reshape(-1), usage.reshape(-1), unused.reshape(-1)


def solution(mesh):
    return jax.shard_map(
        functools.partial(local, mesh.shape["mem"], mesh.shape["camp"]),
        mesh=mesh,
        in_specs=(
            P("mem", None, "camp"),
            P("mem", None, "camp"),
            P("mem", "camp"),
            P("mem", "camp"),
            P("mem", "camp"),
            P("camp"),
            P("camp"),
        ),
        out_specs=(P("camp"), P("camp"), P("mem")),
        check_vma=False,
    )
```

```python
import functools
import math

import jax
import jax.numpy as jnp
from jax import lax
from jax.experimental import pallas as pl
from jax.experimental.pallas import tpu as pltpu
from jax.sharding import PartitionSpec as P

MB = 8
ROUNDS = 3
SMOOTHING = 0.05
STEP_SIZE = 0.2
SCALE = math.log2(math.e) / SMOOTHING
MESH = pl.DeviceIdType.MESH
UNROLL = 20


def flip(i, d):
    out, bit = i, 1
    while bit <= d:
        if d & bit:
            out = out + bit - 2 * bit * lax.rem(lax.div(i, bit), 2)
        bit *= 2
    return out


def kernel(
    n_mem, n_camp, plane,
    gains, costs, rows_in, cols_in, count_in, duals, allowances,
    price, usage, spare,
    g_raw, c_raw, gain, cost, score, run, exp_cost, top_of, weight_of,
    pair, ids, picked, onehot, own_hot, parts, allow,
    own_id, own_price, own_allow, rows, cols, count, prev, last,
    load_sem, z_send, z_recv, p_send, p_recv, c_send, c_recv,
):
    slots, tile = gain.shape[0], gain.shape[1]
    blocks = price.shape[0]
    me = lax.axis_index("mem")
    me_c = lax.axis_index("camp")
    deep = n_mem // plane
    z, b = lax.div(me, plane), lax.rem(me, plane)

    loads = [
        pltpu.make_async_copy(src, dst, load_sem.at[i])
        for i, (src, dst) in enumerate(
            (
                (rows_in, rows), (cols_in, cols), (count_in, count),
                (duals, price), (allowances, allow), (gains, g_raw), (costs, c_raw),
            )
        )
    ]
    for load in loads:
        load.start()

    def z_peer(d):
        return {"mem": flip(z, d) * plane + b, "camp": me_c}

    def p_peer(e):
        return {"mem": z * plane + flip(b, e), "camp": me_c}

    def c_peer(f):
        return {"mem": me, "camp": lax.rem(me_c + f, n_camp)}

    def owner(d, e):
        return flip(z, d) * plane + flip(b, e)

    barrier = pltpu.get_barrier_semaphore()
    peers = (
        [z_peer(d) for d in range(1, deep)]
        + [p_peer(e) for e in range(1, plane)]
        + [c_peer(f) for f in range(1, n_camp)]
    )
    for peer in peers:
        pl.semaphore_signal(barrier, inc=1, device_id=peer, device_id_type=MESH)

    for load in loads[:3]:
        load.wait()
    id_rows = ids.shape[1]
    spot = lax.broadcasted_iota(jnp.int32, (id_rows, tile), 0) * tile
    spot = spot + lax.broadcasted_iota(jnp.int32, (id_rows, tile), 1) - me * slots

    def link(s, carry):
        lasts, packed = carry
        row = rows[0, s]
        live = s < count[0, 0]
        before = jnp.int32(0)
        after = []
        for k in range(MB):
            mine = row == k
            before = jnp.where(mine, lasts[k], before)
            after.append(jnp.where(mine & live, s + 1, lasts[k]))
        prev[s] = before
        block = jnp.where(live, cols[0, s] + 1, 0)
        own_id[pl.ds(s, 1), :] = jnp.full((1, tile), block, jnp.int32)
        return tuple(after), jnp.where(spot == s, block, packed)

    lasts, packed_ids = lax.fori_loop(
        0, slots, link, ((jnp.int32(0),) * MB, jnp.zeros((id_rows, tile), jnp.int32)), unroll=4
    )
    ids[me] = packed_ids
    for k in range(MB):
        last[k] = lasts[k]
    run[0] = jnp.zeros((tile, tile), jnp.float32)

    def z_copy(buf, t, d):
        return pltpu.make_async_remote_copy(
            buf.at[me], buf.at[me], z_send.at[t, d], z_recv.at[t, d], z_peer(d), MESH
        )

    def p_copy(buf, t, d, e):
        block = buf.at[owner(d, 0)]
        return pltpu.make_async_remote_copy(
            block, block, p_send.at[t, d, e], p_recv.at[t, d, e], p_peer(e), MESH
        )

    def gather_start(buf, t):
        for d in range(1, deep):
            z_copy(buf, t, d).start()
        for e in range(1, plane):
            p_copy(buf, t, 0, e).start()

    def gather_relay(buf, t):
        for d in range(1, deep):
            block = buf.at[owner(d, 0)]
            pltpu.make_async_remote_copy(
                block, block, z_send.at[t, d], z_recv.at[t, d], z_peer(d), MESH
            ).wait_recv()
            for e in range(1, plane):
                p_copy(buf, t, d, e).start()

    def gather_wait(buf, t, d):
        for e in range(1, plane):
            block = buf.at[owner(d, e)]
            pltpu.make_async_remote_copy(
                block, block, p_send.at[t, d, e], p_recv.at[t, d, e], p_peer(e), MESH
            ).wait_recv()

    def gather_drain(buf, t):
        for d in range(1, deep):
            z_copy(buf, t, d).wait_send()
        for d in range(deep):
            for e in range(1, plane):
                p_copy(buf, t, d, e).wait_send()

    loads[3].wait()
    loads[4].wait()

    def fetch(s, _):
        here = pl.ds(cols[0, s], 1)
        own_price[pl.ds(s, 1), :] = price[here, :]
        own_allow[pl.ds(s, 1), :] = allow[here, :]
        return 0

    lax.fori_loop(0, slots, fetch, 0, unroll=UNROLL)
    loads[5].wait()
    loads[6].wait()
    lane = lax.broadcasted_iota(jnp.int32, (tile, tile), 1)

    def camp_copy(t, f):
        return pltpu.make_async_remote_copy(
            pair.at[t, me_c], pair.at[t, me_c], c_send.at[t, f], c_recv.at[t, f], c_peer(f), MESH
        )

    def mark():
        packed = ids[0]
        for p in range(1, n_mem):
            packed = packed + ids[p]
        for i in range(n_mem * slots // tile):
            id_row = packed[i : i + 1, :]
            own_hot[:, i * tile : (i + 1) * tile] = jnp.where(
                own_id[...] == id_row, 1.0, 0.0
            ).astype(jnp.bfloat16)
            for j in range(blocks // tile):
                here = lax.broadcasted_iota(jnp.int32, (tile, tile), 0) + (j * tile + 1)
                onehot[j * tile : (j + 1) * tile, i * tile : (i + 1) * tile] = jnp.where(
                    here == id_row, 1.0, 0.0
                ).astype(jnp.bfloat16)

    def summed_by(hot):
        three = jnp.dot(hot, parts[...], preferred_element_type=jnp.float32)
        return three[:, :tile] + three[:, tile : 2 * tile] + three[:, 2 * tile :]

    def advance(price, used, allow):
        return jnp.maximum(price + STEP_SIZE * (used - allow), 0.0)

    def dense():
        now = summed_by(onehot[...])
        usage[...] = now
        price[...] = advance(price[...], now, allow[...])

    for t in range(ROUNDS):
        def scores(s, _):
            row_price = own_price[pl.ds(s, 1), :] * SCALE
            if t == 0:
                worth = g_raw[s].astype(jnp.float32) * SCALE
                drawn = c_raw[s].astype(jnp.float32)
                gain[s] = worth
                cost[s] = drawn
            else:
                worth, drawn = gain[s], cost[s]
            now = worth - drawn * row_price
            score[s] = now
            run[s + 1] = jnp.maximum(run[prev[s]], now)
            return 0

        lax.fori_loop(0, slots, scores, 0, unroll=UNROLL)
        if t == 0:
            pl.semaphore_wait(barrier, len(peers))
            gather_start(ids, 0)

        def tops(k, packed):
            top = jnp.max(run[last[k]], axis=1, keepdims=True)
            top = jnp.broadcast_to(top, (tile, tile))
            top_of[k] = top
            return jnp.where(lane == k, top, packed)

        packed = lax.fori_loop(0, MB, tops, jnp.zeros((tile, tile), jnp.float32), unroll=MB)

        def exponents(s, _):
            now = jnp.exp2(score[s] - top_of[rows[0, s]])
            exp_cost[s] = now * cost[s]
            run[s + 1] = run[prev[s]] + now
            return 0

        lax.fori_loop(0, slots, exponents, 0, unroll=UNROLL)

        def sums(k, packed):
            total = jnp.sum(run[last[k]], axis=1, keepdims=True)
            return jnp.where(lane == k + MB, total, packed)

        packed = lax.fori_loop(0, MB, sums, packed, unroll=MB)
        pair[t, me_c] = jnp.transpose(packed)[: 2 * MB]
        for f in range(1, n_camp):
            camp_copy(t, f).start()

        if t == 0:
            gather_relay(ids, 0)

        for f in range(1, n_camp):
            block = pair.at[t, lax.rem(me_c - f + n_camp, n_camp)]
            pltpu.make_async_remote_copy(
                block, block, c_send.at[t, f], c_recv.at[t, f], c_peer(f), MESH
            ).wait_recv()

        mine = pair[t, me_c, :MB]
        top = pair[t, 0, :MB]
        for c in range(1, n_camp):
            top = jnp.maximum(top, pair[t, c, :MB])
        denom = jnp.zeros((MB, tile), jnp.float32)
        for c in range(n_camp):
            denom = denom + jnp.exp2(pair[t, c, :MB] - top) * pair[t, c, MB:]
        left = jnp.exp2(-top)
        denom = left + denom
        weight = jnp.exp2(mine - top) / denom
        if t == ROUNDS - 1:
            spare[...] = left / denom
        weight = jnp.transpose(jnp.concatenate([weight] * (tile // MB), axis=0))
        for k in range(MB):
            weight_of[k] = jnp.broadcast_to(weight[:, k : k + 1], (tile, tile))

        def uses(s, _):
            used = jnp.sum(exp_cost[s] * weight_of[rows[0, s]], axis=0, keepdims=True)
            picked[t, me, pl.ds(s, 1), :] = used
            return 0

        lax.fori_loop(0, slots, uses, 0, unroll=UNROLL)
        place = lax.broadcasted_iota(jnp.int32, (slots, tile), 0)
        picked[t, me] = jnp.where(place < count[0, 0], picked[t, me], 0.0)

        gather_start(picked.at[t], t + 1)
        gather_relay(picked.at[t], t + 1)
        if t == 0:
            for d in range(deep):
                gather_wait(ids, 0, d)
            mark()
        else:
            dense()
        for d in range(deep):
            gather_wait(picked.at[t], t + 1, d)
            level = flip(z, d)
            rest = picked[t, pl.ds(level * plane, plane)].reshape(plane * slots, tile)
            here = pl.ds(pl.multiple_of(level * (plane * slots), 32), plane * slots)
            for i in range(3):
                part = rest.astype(jnp.bfloat16)
                parts[here, i * tile : (i + 1) * tile] = part
                rest = rest - part.astype(jnp.float32)

        if t < ROUNDS - 1:
            own_price[...] = advance(own_price[...], summed_by(own_hot[...]), own_allow[...])
        else:
            dense()

    gather_drain(ids, 0)
    for t in range(ROUNDS):
        gather_drain(picked.at[t], t + 1)
        for f in range(1, n_camp):
            camp_copy(t, f).wait_send()


def hand_over(price, usage, spare, price_out, usage_out, unused_out, sem):
    stores = [
        pltpu.make_async_copy(src, dst, sem.at[i])
        for i, (src, dst) in enumerate(
            ((price, price_out), (usage, usage_out), (spare, unused_out))
        )
    ]
    for store in stores:
        store.start()
    for store in stores:
        store.wait()


def local(n_mem, n_camp, gains, costs, tile_rows, tile_cols, tile_count, duals, allowances):
    slots, tile, _ = gains.shape
    blocks = duals.shape[0] // tile
    plane = 4 if n_mem % 4 == 0 else 1
    deep = n_mem // plane
    id_rows = -(-n_mem * slots // (8 * tile)) * 8
    f32, bf16 = jnp.float32, jnp.bfloat16
    anywhere = pl.BlockSpec(memory_space=pl.ANY)
    dma = pltpu.SemaphoreType.DMA
    shapes = ((blocks, tile), (blocks, tile), (MB, tile))
    held = pl.pallas_call(
        functools.partial(kernel, n_mem, n_camp, plane),
        out_shape=tuple(pltpu.VMEM(shape, f32) for shape in shapes),
        in_specs=[anywhere] * 7,
        out_specs=(pl.BlockSpec(memory_space=pltpu.VMEM),) * 3,
        scratch_shapes=[
            pltpu.VMEM((slots, tile, tile), bf16),
            pltpu.VMEM((slots, tile, tile), bf16),
            pltpu.VMEM((slots, tile, tile), f32),
            pltpu.VMEM((slots, tile, tile), f32),
            pltpu.VMEM((slots, tile, tile), f32),
            pltpu.VMEM((slots + 1, tile, tile), f32),
            pltpu.VMEM((slots, tile, tile), f32),
            pltpu.VMEM((MB, tile, tile), f32),
            pltpu.VMEM((MB, tile, tile), f32),
            pltpu.VMEM((ROUNDS, n_camp, 2 * MB, tile), f32),
            pltpu.VMEM((n_mem, id_rows, tile), jnp.int32),
            pltpu.VMEM((ROUNDS, n_mem, slots, tile), f32),
            pltpu.VMEM((blocks, n_mem * slots), bf16),
            pltpu.VMEM((slots, n_mem * slots), bf16),
            pltpu.VMEM((n_mem * slots, 3 * tile), bf16),
            pltpu.VMEM((blocks, tile), f32),
            pltpu.VMEM((slots, tile), jnp.int32),
            pltpu.VMEM((slots, tile), f32),
            pltpu.VMEM((slots, tile), f32),
            pltpu.SMEM((1, slots), jnp.int32),
            pltpu.SMEM((1, slots), jnp.int32),
            pltpu.SMEM((1, 1), jnp.int32),
            pltpu.SMEM((slots,), jnp.int32),
            pltpu.SMEM((MB,), jnp.int32),
            dma((7,)),
            dma((ROUNDS + 1, deep)),
            dma((ROUNDS + 1, deep)),
            dma((ROUNDS + 1, deep, plane)),
            dma((ROUNDS + 1, deep, plane)),
            dma((ROUNDS, n_camp)),
            dma((ROUNDS, n_camp)),
        ],
        compiler_params=pltpu.CompilerParams(
            collective_id=0, has_side_effects=True, vmem_limit_bytes=56 * 1024 * 1024
        ),
    )(
        gains, costs, tile_rows.T, tile_cols.T, tile_count,
        duals.reshape(blocks, tile), allowances.reshape(blocks, tile),
    )
    price, usage, unused = pl.pallas_call(
        hand_over,
        out_shape=tuple(jax.ShapeDtypeStruct(shape, f32) for shape in shapes),
        in_specs=[pl.BlockSpec(memory_space=pltpu.VMEM)] * 3,
        out_specs=(anywhere,) * 3,
        scratch_shapes=[dma((3,))],
        compiler_params=pltpu.CompilerParams(vmem_limit_bytes=1024 * 1024),
    )(*held)
    return price.reshape(-1), usage.reshape(-1), unused.reshape(-1)


def solution(mesh):
    return jax.shard_map(
        functools.partial(local, mesh.shape["mem"], mesh.shape["camp"]),
        mesh=mesh,
        in_specs=(
            P("mem", None, "camp"),
            P("mem", None, "camp"),
            P("mem", "camp"),
            P("mem", "camp"),
            P("mem", "camp"),
            P("camp"),
            P("camp"),
        ),
        out_specs=(P("camp"), P("camp"), P("mem")),
        check_vma=False,
    )
```

```python
import functools
import math

import jax
import jax.numpy as jnp
from jax import lax
from jax.experimental import pallas as pl
from jax.experimental.pallas import tpu as pltpu
from jax.sharding import PartitionSpec as P

MB = 8
ROUNDS = 3
SMOOTHING = 0.05
STEP_SIZE = 0.2
SCALE = math.log2(math.e) / SMOOTHING
MESH = pl.DeviceIdType.MESH
UNROLL = 20


def flip(i, d):
    out, bit = i, 1
    while bit <= d:
        if d & bit:
            out = out + bit - 2 * bit * lax.rem(lax.div(i, bit), 2)
        bit *= 2
    return out


def kernel(
    n_mem, n_camp, plane,
    gains, costs, rows_in, cols_in, count_in, duals, allowances,
    price, usage, spare,
    g_raw, c_raw, gain, cost, score, run, exp_cost, top_of, weight_of,
    pair, ids, picked, onehot, own_hot, parts, allow,
    own_id, own_price, own_allow, rows, cols, count, prev, last,
    load_sem, z_send, z_recv, p_send, p_recv, c_send, c_recv,
):
    slots, tile = gain.shape[0], gain.shape[1]
    blocks = price.shape[0]
    me = lax.axis_index("mem")
    me_c = lax.axis_index("camp")
    deep = n_mem // plane
    z, b = lax.div(me, plane), lax.rem(me, plane)

    loads = [
        pltpu.make_async_copy(src, dst, load_sem.at[i])
        for i, (src, dst) in enumerate(
            (
                (rows_in, rows), (cols_in, cols), (count_in, count),
                (duals, price), (allowances, allow), (gains, g_raw), (costs, c_raw),
            )
        )
    ]
    for load in loads:
        load.start()

    level = [flip(z, d) for d in range(deep)]
    place_of = [flip(b, e) for e in range(plane)]
    owners = [[row * plane + column for column in place_of] for row in level]

    def z_peer(d):
        return {"mem": owners[d][0], "camp": me_c}

    def p_peer(e):
        return {"mem": owners[0][e], "camp": me_c}

    def c_peer(f):
        return {"mem": me, "camp": lax.rem(me_c + f, n_camp)}

    barrier = pltpu.get_barrier_semaphore()
    peers = (
        [z_peer(d) for d in range(1, deep)]
        + [p_peer(e) for e in range(1, plane)]
        + [c_peer(f) for f in range(1, n_camp)]
    )
    for peer in peers:
        pl.semaphore_signal(barrier, inc=1, device_id=peer, device_id_type=MESH)

    for load in loads[:3]:
        load.wait()
    id_rows = ids.shape[1]
    spot = lax.broadcasted_iota(jnp.int32, (id_rows, tile), 0) * tile
    spot = spot + lax.broadcasted_iota(jnp.int32, (id_rows, tile), 1) - me * slots

    def link(s, carry):
        lasts, packed = carry
        row = rows[0, s]
        live = s < count[0, 0]
        before = jnp.int32(0)
        after = []
        for k in range(MB):
            mine = row == k
            before = jnp.where(mine, lasts[k], before)
            after.append(jnp.where(mine & live, s + 1, lasts[k]))
        prev[s] = before
        block = jnp.where(live, cols[0, s] + 1, 0)
        own_id[pl.ds(s, 1), :] = jnp.full((1, tile), block, jnp.int32)
        return tuple(after), jnp.where(spot == s, block, packed)

    lasts, packed_ids = lax.fori_loop(
        0, slots, link, ((jnp.int32(0),) * MB, jnp.zeros((id_rows, tile), jnp.int32)), unroll=4
    )
    ids[me] = packed_ids
    for k in range(MB):
        last[k] = lasts[k]
    run[0] = jnp.zeros((tile, tile), jnp.float32)

    def z_copy(buf, t, d):
        return pltpu.make_async_remote_copy(
            buf.at[me], buf.at[me], z_send.at[t, d], z_recv.at[t, d], z_peer(d), MESH
        )

    def p_copy(buf, t, d, e, column=0, to=None):
        block = buf.at[owners[d][column]]
        return pltpu.make_async_remote_copy(
            block, block, p_send.at[t, d, e], p_recv.at[t, d, e], p_peer(to or e), MESH
        )

    def via(d):
        return 1 + d % 2 if plane == 4 and d < deep - 1 else 0

    def p_start(buf, t, d):
        for e in range(1, plane):
            if e < 3 or not via(d):
                p_copy(buf, t, d, e).start()

    def p_wait(buf, t, d, e):
        p_copy(buf, t, d, e, column=e).wait_recv()

    def p_forward(buf, t, d):
        if via(d):
            p_wait(buf, t, d, 3 - via(d))
            p_copy(buf, t, d, 3, column=3 - via(d), to=via(d)).start()

    def gather_start(buf, t):
        for d in range(1, deep):
            z_copy(buf, t, d).start()
        p_start(buf, t, 0)

    def gather_relay(buf, t):
        for d in range(1, deep):
            block = buf.at[owners[d][0]]
            pltpu.make_async_remote_copy(
                block, block, z_send.at[t, d], z_recv.at[t, d], z_peer(d), MESH
            ).wait_recv()
            p_start(buf, t, d)
            p_forward(buf, t, d - 1)

    def gather_wait(buf, t, d):
        for e in range(1, plane):
            if not (via(d) and e == 3 - via(d)):
                p_wait(buf, t, d, e)

    def gather_drain(buf, t):
        for d in range(1, deep):
            z_copy(buf, t, d).wait_send()
        for d in range(deep):
            for e in range(1, plane):
                p_copy(buf, t, d, e).wait_send()

    loads[3].wait()
    loads[4].wait()

    def fetch(s, _):
        here = pl.ds(cols[0, s], 1)
        own_price[pl.ds(s, 1), :] = price[here, :]
        own_allow[pl.ds(s, 1), :] = allow[here, :]
        return 0

    lax.fori_loop(0, slots, fetch, 0, unroll=UNROLL)
    loads[5].wait()
    loads[6].wait()
    lane = lax.broadcasted_iota(jnp.int32, (tile, tile), 1)

    def camp_copy(t, f):
        return pltpu.make_async_remote_copy(
            pair.at[t, me_c], pair.at[t, me_c], c_send.at[t, f], c_recv.at[t, f], c_peer(f), MESH
        )

    def mark():
        packed = ids[0]
        for p in range(1, n_mem):
            packed = packed + ids[p]
        for i in range(n_mem * slots // tile):
            id_row = packed[i : i + 1, :]
            own_hot[:, i * tile : (i + 1) * tile] = jnp.where(
                own_id[...] == id_row, 1.0, 0.0
            ).astype(jnp.bfloat16)
            for j in range(blocks // tile):
                here = lax.broadcasted_iota(jnp.int32, (tile, tile), 0) + (j * tile + 1)
                onehot[j * tile : (j + 1) * tile, i * tile : (i + 1) * tile] = jnp.where(
                    here == id_row, 1.0, 0.0
                ).astype(jnp.bfloat16)

    def summed_by(hot):
        three = jnp.dot(hot, parts[...], preferred_element_type=jnp.float32)
        return three[:, :tile] + three[:, tile : 2 * tile] + three[:, 2 * tile :]

    def advance(price, used, allow):
        return jnp.maximum(price + STEP_SIZE * (used - allow), 0.0)

    def dense():
        now = summed_by(onehot[...])
        usage[...] = now
        price[...] = advance(price[...], now, allow[...])

    for t in range(ROUNDS):
        def scores(s, _):
            row_price = own_price[pl.ds(s, 1), :] * SCALE
            if t == 0:
                worth = g_raw[s].astype(jnp.float32) * SCALE
                drawn = c_raw[s].astype(jnp.float32)
                gain[s] = worth
                cost[s] = drawn
            else:
                worth, drawn = gain[s], cost[s]
            now = worth - drawn * row_price
            score[s] = now
            run[s + 1] = jnp.maximum(run[prev[s]], now)
            return 0

        lax.fori_loop(0, slots, scores, 0, unroll=UNROLL)
        if t == 0:
            pl.semaphore_wait(barrier, len(peers))
            gather_start(ids, 0)

        def tops(k, packed):
            top = jnp.max(run[last[k]], axis=1, keepdims=True)
            top = jnp.broadcast_to(top, (tile, tile))
            top_of[k] = top
            return jnp.where(lane == k, top, packed)

        packed = lax.fori_loop(0, MB, tops, jnp.zeros((tile, tile), jnp.float32), unroll=MB)

        def exponents(s, _):
            now = jnp.exp2(score[s] - top_of[rows[0, s]])
            exp_cost[s] = now * cost[s]
            run[s + 1] = run[prev[s]] + now
            return 0

        lax.fori_loop(0, slots, exponents, 0, unroll=UNROLL)

        def sums(k, packed):
            total = jnp.sum(run[last[k]], axis=1, keepdims=True)
            return jnp.where(lane == k + MB, total, packed)

        packed = lax.fori_loop(0, MB, sums, packed, unroll=MB)
        pair[t, me_c] = jnp.transpose(packed)[: 2 * MB]
        for f in range(1, n_camp):
            camp_copy(t, f).start()

        if t == 0:
            gather_relay(ids, 0)

        for f in range(1, n_camp):
            block = pair.at[t, lax.rem(me_c - f + n_camp, n_camp)]
            pltpu.make_async_remote_copy(
                block, block, c_send.at[t, f], c_recv.at[t, f], c_peer(f), MESH
            ).wait_recv()

        mine = pair[t, me_c, :MB]
        top = pair[t, 0, :MB]
        for c in range(1, n_camp):
            top = jnp.maximum(top, pair[t, c, :MB])
        denom = jnp.zeros((MB, tile), jnp.float32)
        for c in range(n_camp):
            denom = denom + jnp.exp2(pair[t, c, :MB] - top) * pair[t, c, MB:]
        left = jnp.exp2(-top)
        denom = left + denom
        weight = jnp.exp2(mine - top) / denom
        if t == ROUNDS - 1:
            spare[...] = left / denom
        weight = jnp.transpose(jnp.concatenate([weight] * (tile // MB), axis=0))
        for k in range(MB):
            weight_of[k] = jnp.broadcast_to(weight[:, k : k + 1], (tile, tile))

        def uses(s, _):
            used = jnp.sum(exp_cost[s] * weight_of[rows[0, s]], axis=0, keepdims=True)
            picked[t, me, pl.ds(s, 1), :] = used
            return 0

        lax.fori_loop(0, slots, uses, 0, unroll=UNROLL)
        place = lax.broadcasted_iota(jnp.int32, (slots, tile), 0)
        picked[t, me] = jnp.where(place < count[0, 0], picked[t, me], 0.0)

        gather_start(picked.at[t], t + 1)
        gather_relay(picked.at[t], t + 1)
        if t == 0:
            for d in range(deep):
                gather_wait(ids, 0, d)
            mark()
        else:
            dense()
        for d in range(deep):
            gather_wait(picked.at[t], t + 1, d)
            rest = picked[t, pl.ds(level[d] * plane, plane)].reshape(plane * slots, tile)
            here = pl.ds(pl.multiple_of(level[d] * (plane * slots), 32), plane * slots)
            for i in range(3):
                part = rest.astype(jnp.bfloat16)
                parts[here, i * tile : (i + 1) * tile] = part
                rest = rest - part.astype(jnp.float32)

        if t < ROUNDS - 1:
            own_price[...] = advance(own_price[...], summed_by(own_hot[...]), own_allow[...])
        else:
            dense()

    gather_drain(ids, 0)
    for t in range(ROUNDS):
        gather_drain(picked.at[t], t + 1)
        for f in range(1, n_camp):
            camp_copy(t, f).wait_send()


def hand_over(price, usage, spare, price_out, usage_out, unused_out, sem):
    stores = [
        pltpu.make_async_copy(src, dst, sem.at[i])
        for i, (src, dst) in enumerate(
            ((price, price_out), (usage, usage_out), (spare, unused_out))
        )
    ]
    for store in stores:
        store.start()
    for store in stores:
        store.wait()


def local(n_mem, n_camp, gains, costs, tile_rows, tile_cols, tile_count, duals, allowances):
    slots, tile, _ = gains.shape
    blocks = duals.shape[0] // tile
    plane = 4 if n_mem % 4 == 0 else 1
    deep = n_mem // plane
    id_rows = -(-n_mem * slots // (8 * tile)) * 8
    f32, bf16 = jnp.float32, jnp.bfloat16
    anywhere = pl.BlockSpec(memory_space=pl.ANY)
    dma = pltpu.SemaphoreType.DMA
    shapes = ((blocks, tile), (blocks, tile), (MB, tile))
    held = pl.pallas_call(
        functools.partial(kernel, n_mem, n_camp, plane),
        out_shape=tuple(pltpu.VMEM(shape, f32) for shape in shapes),
        in_specs=[anywhere] * 7,
        out_specs=(pl.BlockSpec(memory_space=pltpu.VMEM),) * 3,
        scratch_shapes=[
            pltpu.VMEM((slots, tile, tile), bf16),
            pltpu.VMEM((slots, tile, tile), bf16),
            pltpu.VMEM((slots, tile, tile), f32),
            pltpu.VMEM((slots, tile, tile), f32),
            pltpu.VMEM((slots, tile, tile), f32),
            pltpu.VMEM((slots + 1, tile, tile), f32),
            pltpu.VMEM((slots, tile, tile), f32),
            pltpu.VMEM((MB, tile, tile), f32),
            pltpu.VMEM((MB, tile, tile), f32),
            pltpu.VMEM((ROUNDS, n_camp, 2 * MB, tile), f32),
            pltpu.VMEM((n_mem, id_rows, tile), jnp.int32),
            pltpu.VMEM((ROUNDS, n_mem, slots, tile), f32),
            pltpu.VMEM((blocks, n_mem * slots), bf16),
            pltpu.VMEM((slots, n_mem * slots), bf16),
            pltpu.VMEM((n_mem * slots, 3 * tile), bf16),
            pltpu.VMEM((blocks, tile), f32),
            pltpu.VMEM((slots, tile), jnp.int32),
            pltpu.VMEM((slots, tile), f32),
            pltpu.VMEM((slots, tile), f32),
            pltpu.SMEM((1, slots), jnp.int32),
            pltpu.SMEM((1, slots), jnp.int32),
            pltpu.SMEM((1, 1), jnp.int32),
            pltpu.SMEM((slots,), jnp.int32),
            pltpu.SMEM((MB,), jnp.int32),
            dma((7,)),
            dma((ROUNDS + 1, deep)),
            dma((ROUNDS + 1, deep)),
            dma((ROUNDS + 1, deep, plane)),
            dma((ROUNDS + 1, deep, plane)),
            dma((ROUNDS, n_camp)),
            dma((ROUNDS, n_camp)),
        ],
        compiler_params=pltpu.CompilerParams(
            collective_id=0, has_side_effects=True, vmem_limit_bytes=56 * 1024 * 1024
        ),
    )(
        gains, costs, tile_rows.T, tile_cols.T, tile_count,
        duals.reshape(blocks, tile), allowances.reshape(blocks, tile),
    )
    price, usage, unused = pl.pallas_call(
        hand_over,
        out_shape=tuple(jax.ShapeDtypeStruct(shape, f32) for shape in shapes),
        in_specs=[pl.BlockSpec(memory_space=pltpu.VMEM)] * 3,
        out_specs=(anywhere,) * 3,
        scratch_shapes=[dma((3,))],
        compiler_params=pltpu.CompilerParams(vmem_limit_bytes=1024 * 1024),
    )(*held)
    return price.reshape(-1), usage.reshape(-1), unused.reshape(-1)


def solution(mesh):
    return jax.shard_map(
        functools.partial(local, mesh.shape["mem"], mesh.shape["camp"]),
        mesh=mesh,
        in_specs=(
            P("mem", None, "camp"),
            P("mem", None, "camp"),
            P("mem", "camp"),
            P("mem", "camp"),
            P("mem", "camp"),
            P("camp"),
            P("camp"),
        ),
        out_specs=(P("camp"), P("camp"), P("mem")),
        check_vma=False,
    )
```

```python
import functools
import math

import jax
import jax.numpy as jnp
from jax import lax
from jax.experimental import pallas as pl
from jax.experimental.pallas import tpu as pltpu
from jax.sharding import PartitionSpec as P

MB = 8
ROUNDS = 3
SMOOTHING = 0.05
STEP_SIZE = 0.2
SCALE = math.log2(math.e) / SMOOTHING
MESH = pl.DeviceIdType.MESH
UNROLL = 20


def flip(i, d):
    out, bit = i, 1
    while bit <= d:
        if d & bit:
            out = out + bit - 2 * bit * lax.rem(lax.div(i, bit), 2)
        bit *= 2
    return out


def kernel(
    n_mem, n_camp, plane,
    gains, costs, rows_in, cols_in, count_in, duals, allowances,
    price, usage, spare,
    g_raw, c_raw, gain, cost, score, run, exp_cost, top_of, weight_of,
    pair, ids, picked, onehot, own_hot, parts, allow,
    own_id, own_price, own_allow, rows, cols, count, prev, last,
    load_sem, z_send, z_recv, p_send, p_recv, c_send, c_recv,
):
    slots, tile = gain.shape[0], gain.shape[1]
    blocks = price.shape[0]
    me = lax.axis_index("mem")
    me_c = lax.axis_index("camp")
    deep = n_mem // plane
    z, b = lax.div(me, plane), lax.rem(me, plane)

    loads = [
        pltpu.make_async_copy(src, dst, load_sem.at[i])
        for i, (src, dst) in enumerate(
            (
                (rows_in, rows), (cols_in, cols), (count_in, count),
                (duals, price), (allowances, allow), (gains, g_raw), (costs, c_raw),
            )
        )
    ]
    for load in loads:
        load.start()

    direct = range(1, min(2, deep))
    level = [flip(z, d) for d in range(deep)]
    place_of = [flip(b, e) for e in range(plane)]
    owners = [[row * plane + column for column in place_of] for row in level]

    def z_peer(d):
        return {"mem": owners[d][0], "camp": me_c}

    def p_peer(e):
        return {"mem": owners[0][e], "camp": me_c}

    def d_peer(d, e):
        return {"mem": owners[d][e], "camp": me_c}

    def c_peer(f):
        return {"mem": me, "camp": lax.rem(me_c + f, n_camp)}

    barrier = pltpu.get_barrier_semaphore()
    peers = (
        [z_peer(d) for d in range(1, deep)]
        + [p_peer(e) for e in range(1, plane)]
        + [d_peer(d, e) for d in direct for e in range(1, plane)]
        + [c_peer(f) for f in range(1, n_camp)]
    )
    for peer in peers:
        pl.semaphore_signal(barrier, inc=1, device_id=peer, device_id_type=MESH)

    for load in loads[:3]:
        load.wait()
    id_rows = ids.shape[1]
    spot = lax.broadcasted_iota(jnp.int32, (id_rows, tile), 0) * tile
    spot = spot + lax.broadcasted_iota(jnp.int32, (id_rows, tile), 1) - me * slots

    def link(s, carry):
        lasts, packed = carry
        row = rows[0, s]
        live = s < count[0, 0]
        before = jnp.int32(0)
        after = []
        for k in range(MB):
            mine = row == k
            before = jnp.where(mine, lasts[k], before)
            after.append(jnp.where(mine & live, s + 1, lasts[k]))
        prev[s] = before
        block = jnp.where(live, cols[0, s] + 1, 0)
        own_id[pl.ds(s, 1), :] = jnp.full((1, tile), block, jnp.int32)
        return tuple(after), jnp.where(spot == s, block, packed)

    lasts, packed_ids = lax.fori_loop(
        0, slots, link, ((jnp.int32(0),) * MB, jnp.zeros((id_rows, tile), jnp.int32)), unroll=4
    )
    ids[me] = packed_ids
    for k in range(MB):
        last[k] = lasts[k]
    run[0] = jnp.zeros((tile, tile), jnp.float32)

    def z_copy(buf, t, d):
        return pltpu.make_async_remote_copy(
            buf.at[me], buf.at[me], z_send.at[t, d], z_recv.at[t, d], z_peer(d), MESH
        )

    def p_copy(buf, t, d, e, block, peer):
        block = buf.at[block]
        return pltpu.make_async_remote_copy(
            block, block, p_send.at[t, d, e], p_recv.at[t, d, e], peer, MESH
        )

    def z_wait(buf, t, d):
        block = buf.at[owners[d][0]]
        pltpu.make_async_remote_copy(
            block, block, z_send.at[t, d], z_recv.at[t, d], z_peer(d), MESH
        ).wait_recv()

    def gather_start(buf, t):
        for d in reversed(range(1, deep)):
            z_copy(buf, t, d).start()
        for e in range(1, plane):
            p_copy(buf, t, 0, e, me, p_peer(e)).start()
        for d in direct:
            for e in range(1, plane):
                p_copy(buf, t, d, e, me, d_peer(d, e)).start()

    def gather_relay(buf, t):
        for d in range(len(direct) + 1, deep):
            z_wait(buf, t, d)
            for e in range(1, plane):
                p_copy(buf, t, d, e, owners[d][0], p_peer(e)).start()

    def gather_wait(buf, t, d):
        if d in direct:
            z_wait(buf, t, d)
        for e in range(1, plane):
            p_copy(buf, t, d, e, owners[d][e], p_peer(e)).wait_recv()

    def gather_drain(buf, t):
        for d in range(1, deep):
            z_copy(buf, t, d).wait_send()
        for d in range(deep):
            for e in range(1, plane):
                p_copy(buf, t, d, e, me, p_peer(e)).wait_send()

    loads[3].wait()
    loads[4].wait()

    def fetch(s, _):
        here = pl.ds(cols[0, s], 1)
        own_price[pl.ds(s, 1), :] = price[here, :]
        own_allow[pl.ds(s, 1), :] = allow[here, :]
        return 0

    lax.fori_loop(0, slots, fetch, 0, unroll=UNROLL)
    loads[5].wait()
    loads[6].wait()
    lane = lax.broadcasted_iota(jnp.int32, (tile, tile), 1)

    def camp_copy(t, f):
        return pltpu.make_async_remote_copy(
            pair.at[t, me_c], pair.at[t, me_c], c_send.at[t, f], c_recv.at[t, f], c_peer(f), MESH
        )

    def mark():
        packed = ids[0]
        for p in range(1, n_mem):
            packed = packed + ids[p]
        for i in range(n_mem * slots // tile):
            id_row = packed[i : i + 1, :]
            own_hot[:, i * tile : (i + 1) * tile] = jnp.where(
                own_id[...] == id_row, 1.0, 0.0
            ).astype(jnp.bfloat16)
            for j in range(blocks // tile):
                here = lax.broadcasted_iota(jnp.int32, (tile, tile), 0) + (j * tile + 1)
                onehot[j * tile : (j + 1) * tile, i * tile : (i + 1) * tile] = jnp.where(
                    here == id_row, 1.0, 0.0
                ).astype(jnp.bfloat16)

    def summed_by(hot):
        three = jnp.dot(hot, parts[...], preferred_element_type=jnp.float32)
        return three[:, :tile] + three[:, tile : 2 * tile] + three[:, 2 * tile :]

    def advance(price, used, allow):
        return jnp.maximum(price + STEP_SIZE * (used - allow), 0.0)

    def dense():
        now = summed_by(onehot[...])
        usage[...] = now
        price[...] = advance(price[...], now, allow[...])

    for t in range(ROUNDS):
        def scores(s, _):
            row_price = own_price[pl.ds(s, 1), :] * SCALE
            if t == 0:
                worth = g_raw[s].astype(jnp.float32) * SCALE
                drawn = c_raw[s].astype(jnp.float32)
                gain[s] = worth
                cost[s] = drawn
            else:
                worth, drawn = gain[s], cost[s]
            now = worth - drawn * row_price
            score[s] = now
            run[s + 1] = jnp.maximum(run[prev[s]], now)
            return 0

        lax.fori_loop(0, slots, scores, 0, unroll=UNROLL)
        if t == 0:
            pl.semaphore_wait(barrier, len(peers))
            gather_start(ids, 0)

        def tops(k, packed):
            top = jnp.max(run[last[k]], axis=1, keepdims=True)
            top = jnp.broadcast_to(top, (tile, tile))
            top_of[k] = top
            return jnp.where(lane == k, top, packed)

        packed = lax.fori_loop(0, MB, tops, jnp.zeros((tile, tile), jnp.float32), unroll=MB)

        def exponents(s, _):
            now = jnp.exp2(score[s] - top_of[rows[0, s]])
            exp_cost[s] = now * cost[s]
            run[s + 1] = run[prev[s]] + now
            return 0

        lax.fori_loop(0, slots, exponents, 0, unroll=UNROLL)

        def sums(k, packed):
            total = jnp.sum(run[last[k]], axis=1, keepdims=True)
            return jnp.where(lane == k + MB, total, packed)

        packed = lax.fori_loop(0, MB, sums, packed, unroll=MB)
        pair[t, me_c] = jnp.transpose(packed)[: 2 * MB]
        for f in range(1, n_camp):
            camp_copy(t, f).start()

        if t == 0:
            gather_relay(ids, 0)

        for f in range(1, n_camp):
            block = pair.at[t, lax.rem(me_c - f + n_camp, n_camp)]
            pltpu.make_async_remote_copy(
                block, block, c_send.at[t, f], c_recv.at[t, f], c_peer(f), MESH
            ).wait_recv()

        mine = pair[t, me_c, :MB]
        top = pair[t, 0, :MB]
        for c in range(1, n_camp):
            top = jnp.maximum(top, pair[t, c, :MB])
        denom = jnp.zeros((MB, tile), jnp.float32)
        for c in range(n_camp):
            denom = denom + jnp.exp2(pair[t, c, :MB] - top) * pair[t, c, MB:]
        left = jnp.exp2(-top)
        denom = left + denom
        weight = jnp.exp2(mine - top) / denom
        if t == ROUNDS - 1:
            spare[...] = left / denom
        weight = jnp.transpose(jnp.concatenate([weight] * (tile // MB), axis=0))
        for k in range(MB):
            weight_of[k] = jnp.broadcast_to(weight[:, k : k + 1], (tile, tile))

        def uses(s, _):
            used = jnp.sum(exp_cost[s] * weight_of[rows[0, s]], axis=0, keepdims=True)
            picked[t, me, pl.ds(s, 1), :] = used
            return 0

        lax.fori_loop(0, slots, uses, 0, unroll=UNROLL)
        place = lax.broadcasted_iota(jnp.int32, (slots, tile), 0)
        picked[t, me] = jnp.where(place < count[0, 0], picked[t, me], 0.0)

        gather_start(picked.at[t], t + 1)
        gather_relay(picked.at[t], t + 1)
        if t == 0:
            for d in range(deep):
                gather_wait(ids, 0, d)
            mark()
        else:
            dense()
        for d in range(deep):
            gather_wait(picked.at[t], t + 1, d)
            rest = picked[t, pl.ds(level[d] * plane, plane)].reshape(plane * slots, tile)
            here = pl.ds(pl.multiple_of(level[d] * (plane * slots), 32), plane * slots)
            for i in range(3):
                part = rest.astype(jnp.bfloat16)
                parts[here, i * tile : (i + 1) * tile] = part
                rest = rest - part.astype(jnp.float32)

        if t < ROUNDS - 1:
            own_price[...] = advance(own_price[...], summed_by(own_hot[...]), own_allow[...])
        else:
            dense()

    gather_drain(ids, 0)
    for t in range(ROUNDS):
        gather_drain(picked.at[t], t + 1)
        for f in range(1, n_camp):
            camp_copy(t, f).wait_send()


def hand_over(price, usage, spare, price_out, usage_out, unused_out, sem):
    stores = [
        pltpu.make_async_copy(src, dst, sem.at[i])
        for i, (src, dst) in enumerate(
            ((price, price_out), (usage, usage_out), (spare, unused_out))
        )
    ]
    for store in stores:
        store.start()
    for store in stores:
        store.wait()


def local(n_mem, n_camp, gains, costs, tile_rows, tile_cols, tile_count, duals, allowances):
    slots, tile, _ = gains.shape
    blocks = duals.shape[0] // tile
    plane = 4 if n_mem % 4 == 0 else 1
    deep = n_mem // plane
    id_rows = -(-n_mem * slots // (8 * tile)) * 8
    f32, bf16 = jnp.float32, jnp.bfloat16
    anywhere = pl.BlockSpec(memory_space=pl.ANY)
    dma = pltpu.SemaphoreType.DMA
    shapes = ((blocks, tile), (blocks, tile), (MB, tile))
    held = pl.pallas_call(
        functools.partial(kernel, n_mem, n_camp, plane),
        out_shape=tuple(pltpu.VMEM(shape, f32) for shape in shapes),
        in_specs=[anywhere] * 7,
        out_specs=(pl.BlockSpec(memory_space=pltpu.VMEM),) * 3,
        scratch_shapes=[
            pltpu.VMEM((slots, tile, tile), bf16),
            pltpu.VMEM((slots, tile, tile), bf16),
            pltpu.VMEM((slots, tile, tile), f32),
            pltpu.VMEM((slots, tile, tile), f32),
            pltpu.VMEM((slots, tile, tile), f32),
            pltpu.VMEM((slots + 1, tile, tile), f32),
            pltpu.VMEM((slots, tile, tile), f32),
            pltpu.VMEM((MB, tile, tile), f32),
            pltpu.VMEM((MB, tile, tile), f32),
            pltpu.VMEM((ROUNDS, n_camp, 2 * MB, tile), f32),
            pltpu.VMEM((n_mem, id_rows, tile), jnp.int32),
            pltpu.VMEM((ROUNDS, n_mem, slots, tile), f32),
            pltpu.VMEM((blocks, n_mem * slots), bf16),
            pltpu.VMEM((slots, n_mem * slots), bf16),
            pltpu.VMEM((n_mem * slots, 3 * tile), bf16),
            pltpu.VMEM((blocks, tile), f32),
            pltpu.VMEM((slots, tile), jnp.int32),
            pltpu.VMEM((slots, tile), f32),
            pltpu.VMEM((slots, tile), f32),
            pltpu.SMEM((1, slots), jnp.int32),
            pltpu.SMEM((1, slots), jnp.int32),
            pltpu.SMEM((1, 1), jnp.int32),
            pltpu.SMEM((slots,), jnp.int32),
            pltpu.SMEM((MB,), jnp.int32),
            dma((7,)),
            dma((ROUNDS + 1, deep)),
            dma((ROUNDS + 1, deep)),
            dma((ROUNDS + 1, deep, plane)),
            dma((ROUNDS + 1, deep, plane)),
            dma((ROUNDS, n_camp)),
            dma((ROUNDS, n_camp)),
        ],
        compiler_params=pltpu.CompilerParams(
            collective_id=0, has_side_effects=True, vmem_limit_bytes=56 * 1024 * 1024
        ),
    )(
        gains, costs, tile_rows.T, tile_cols.T, tile_count,
        duals.reshape(blocks, tile), allowances.reshape(blocks, tile),
    )
    price, usage, unused = pl.pallas_call(
        hand_over,
        out_shape=tuple(jax.ShapeDtypeStruct(shape, f32) for shape in shapes),
        in_specs=[pl.BlockSpec(memory_space=pltpu.VMEM)] * 3,
        out_specs=(anywhere,) * 3,
        scratch_shapes=[dma((3,))],
        compiler_params=pltpu.CompilerParams(vmem_limit_bytes=1024 * 1024),
    )(*held)
    return price.reshape(-1), usage.reshape(-1), unused.reshape(-1)


def solution(mesh):
    return jax.shard_map(
        functools.partial(local, mesh.shape["mem"], mesh.shape["camp"]),
        mesh=mesh,
        in_specs=(
            P("mem", None, "camp"),
            P("mem", None, "camp"),
            P("mem", "camp"),
            P("mem", "camp"),
            P("mem", "camp"),
            P("camp"),
            P("camp"),
        ),
        out_specs=(P("camp"), P("camp"), P("mem")),
        check_vma=False,
    )
```

```python
import functools
import math

import jax
import jax.numpy as jnp
from jax import lax
from jax.experimental import pallas as pl
from jax.experimental.pallas import tpu as pltpu
from jax.sharding import PartitionSpec as P

MB = 8
ROUNDS = 3
SMOOTHING = 0.05
STEP_SIZE = 0.2
SCALE = math.log2(math.e) / SMOOTHING
MESH = pl.DeviceIdType.MESH
UNROLL = 20


def flip(i, d):
    out, bit = i, 1
    while bit <= d:
        if d & bit:
            out = out + bit - 2 * bit * lax.rem(lax.div(i, bit), 2)
        bit *= 2
    return out


def kernel(
    n_mem, n_camp, plane,
    gains, costs, rows_in, cols_in, count_in, duals, allowances,
    price, usage, spare,
    g_raw, c_raw, gain, cost, score, run, exp_cost, top_of, weight_of,
    pair, ids, picked, onehot, own_hot, parts, allow,
    own_id, own_price, own_allow, rows, cols, count, prev, last,
    load_sem, z_send, z_recv, p_send, p_recv, c_send, c_recv,
):
    slots, tile = gain.shape[0], gain.shape[1]
    blocks = price.shape[0]
    me = lax.axis_index("mem")
    me_c = lax.axis_index("camp")
    deep = n_mem // plane
    z, b = lax.div(me, plane), lax.rem(me, plane)

    loads = [
        pltpu.make_async_copy(src, dst, load_sem.at[i])
        for i, (src, dst) in enumerate(
            (
                (rows_in, rows), (cols_in, cols), (count_in, count),
                (duals, price), (allowances, allow), (gains, g_raw), (costs, c_raw),
            )
        )
    ]
    for load in loads:
        load.start()

    direct = range(1, min(3, deep))
    level = [flip(z, d) for d in range(deep)]
    place_of = [flip(b, e) for e in range(plane)]
    owners = [[row * plane + column for column in place_of] for row in level]

    def z_peer(d):
        return {"mem": owners[d][0], "camp": me_c}

    def p_peer(e):
        return {"mem": owners[0][e], "camp": me_c}

    def d_peer(d, e):
        return {"mem": owners[d][e], "camp": me_c}

    def c_peer(f):
        return {"mem": me, "camp": lax.rem(me_c + f, n_camp)}

    barrier = pltpu.get_barrier_semaphore()
    peers = (
        [z_peer(d) for d in range(1, deep)]
        + [p_peer(e) for e in range(1, plane)]
        + [d_peer(d, e) for d in direct for e in range(1, plane)]
        + [c_peer(f) for f in range(1, n_camp)]
    )
    for peer in peers:
        pl.semaphore_signal(barrier, inc=1, device_id=peer, device_id_type=MESH)

    for load in loads[:3]:
        load.wait()
    id_rows = ids.shape[1]
    spot = lax.broadcasted_iota(jnp.int32, (id_rows, tile), 0) * tile
    spot = spot + lax.broadcasted_iota(jnp.int32, (id_rows, tile), 1) - me * slots

    def link(s, carry):
        lasts, packed = carry
        row = rows[0, s]
        live = s < count[0, 0]
        before = jnp.int32(0)
        after = []
        for k in range(MB):
            mine = row == k
            before = jnp.where(mine, lasts[k], before)
            after.append(jnp.where(mine & live, s + 1, lasts[k]))
        prev[s] = before
        block = jnp.where(live, cols[0, s] + 1, 0)
        own_id[pl.ds(s, 1), :] = jnp.full((1, tile), block, jnp.int32)
        return tuple(after), jnp.where(spot == s, block, packed)

    lasts, packed_ids = lax.fori_loop(
        0, slots, link, ((jnp.int32(0),) * MB, jnp.zeros((id_rows, tile), jnp.int32)), unroll=4
    )
    ids[me] = packed_ids
    for k in range(MB):
        last[k] = lasts[k]
    run[0] = jnp.zeros((tile, tile), jnp.float32)

    def z_copy(buf, t, d):
        return pltpu.make_async_remote_copy(
            buf.at[me], buf.at[me], z_send.at[t, d], z_recv.at[t, d], z_peer(d), MESH
        )

    def p_copy(buf, t, d, e, block, peer):
        block = buf.at[block]
        return pltpu.make_async_remote_copy(
            block, block, p_send.at[t, d, e], p_recv.at[t, d, e], peer, MESH
        )

    def z_wait(buf, t, d):
        block = buf.at[owners[d][0]]
        pltpu.make_async_remote_copy(
            block, block, z_send.at[t, d], z_recv.at[t, d], z_peer(d), MESH
        ).wait_recv()

    def gather_start(buf, t):
        for d in reversed(range(1, deep)):
            z_copy(buf, t, d).start()
        for e in range(1, plane):
            p_copy(buf, t, 0, e, me, p_peer(e)).start()
        for d in direct:
            for e in range(1, plane):
                p_copy(buf, t, d, e, me, d_peer(d, e)).start()

    def gather_relay(buf, t):
        for d in range(len(direct) + 1, deep):
            z_wait(buf, t, d)
            for e in range(1, plane):
                p_copy(buf, t, d, e, owners[d][0], p_peer(e)).start()

    def gather_wait(buf, t, d):
        if d in direct:
            z_wait(buf, t, d)
        for e in range(1, plane):
            p_copy(buf, t, d, e, owners[d][e], p_peer(e)).wait_recv()

    def gather_drain(buf, t):
        for d in range(1, deep):
            z_copy(buf, t, d).wait_send()
        for d in range(deep):
            for e in range(1, plane):
                p_copy(buf, t, d, e, me, p_peer(e)).wait_send()

    loads[3].wait()
    loads[4].wait()

    def fetch(s, _):
        here = pl.ds(cols[0, s], 1)
        own_price[pl.ds(s, 1), :] = price[here, :]
        own_allow[pl.ds(s, 1), :] = allow[here, :]
        return 0

    lax.fori_loop(0, slots, fetch, 0, unroll=UNROLL)
    loads[5].wait()
    loads[6].wait()
    lane = lax.broadcasted_iota(jnp.int32, (tile, tile), 1)

    def camp_copy(t, f):
        return pltpu.make_async_remote_copy(
            pair.at[t, me_c], pair.at[t, me_c], c_send.at[t, f], c_recv.at[t, f], c_peer(f), MESH
        )

    def mark():
        packed = ids[0]
        for p in range(1, n_mem):
            packed = packed + ids[p]
        for i in range(n_mem * slots // tile):
            id_row = packed[i : i + 1, :]
            own_hot[:, i * tile : (i + 1) * tile] = jnp.where(
                own_id[...] == id_row, 1.0, 0.0
            ).astype(jnp.bfloat16)
            for j in range(blocks // tile):
                here = lax.broadcasted_iota(jnp.int32, (tile, tile), 0) + (j * tile + 1)
                onehot[j * tile : (j + 1) * tile, i * tile : (i + 1) * tile] = jnp.where(
                    here == id_row, 1.0, 0.0
                ).astype(jnp.bfloat16)

    def summed_by(hot):
        three = jnp.dot(hot, parts[...], preferred_element_type=jnp.float32)
        return three[:, :tile] + three[:, tile : 2 * tile] + three[:, 2 * tile :]

    def advance(price, used, allow):
        return jnp.maximum(price + STEP_SIZE * (used - allow), 0.0)

    def dense():
        now = summed_by(onehot[...])
        usage[...] = now
        price[...] = advance(price[...], now, allow[...])

    for t in range(ROUNDS):
        def scores(s, _):
            row_price = own_price[pl.ds(s, 1), :] * SCALE
            if t == 0:
                worth = g_raw[s].astype(jnp.float32) * SCALE
                drawn = c_raw[s].astype(jnp.float32)
                gain[s] = worth
                cost[s] = drawn
            else:
                worth, drawn = gain[s], cost[s]
            now = worth - drawn * row_price
            score[s] = now
            run[s + 1] = jnp.maximum(run[prev[s]], now)
            return 0

        lax.fori_loop(0, slots, scores, 0, unroll=UNROLL)
        if t == 0:
            pl.semaphore_wait(barrier, len(peers))
            gather_start(ids, 0)

        def tops(k, packed):
            top = jnp.max(run[last[k]], axis=1, keepdims=True)
            top = jnp.broadcast_to(top, (tile, tile))
            top_of[k] = top
            return jnp.where(lane == k, top, packed)

        packed = lax.fori_loop(0, MB, tops, jnp.zeros((tile, tile), jnp.float32), unroll=MB)

        def exponents(s, _):
            now = jnp.exp2(score[s] - top_of[rows[0, s]])
            exp_cost[s] = now * cost[s]
            run[s + 1] = run[prev[s]] + now
            return 0

        lax.fori_loop(0, slots, exponents, 0, unroll=UNROLL)

        def sums(k, packed):
            total = jnp.sum(run[last[k]], axis=1, keepdims=True)
            return jnp.where(lane == k + MB, total, packed)

        packed = lax.fori_loop(0, MB, sums, packed, unroll=MB)
        pair[t, me_c] = jnp.transpose(packed)[: 2 * MB]
        for f in range(1, n_camp):
            camp_copy(t, f).start()

        if t == 0:
            gather_relay(ids, 0)

        for f in range(1, n_camp):
            block = pair.at[t, lax.rem(me_c - f + n_camp, n_camp)]
            pltpu.make_async_remote_copy(
                block, block, c_send.at[t, f], c_recv.at[t, f], c_peer(f), MESH
            ).wait_recv()

        mine = pair[t, me_c, :MB]
        top = pair[t, 0, :MB]
        for c in range(1, n_camp):
            top = jnp.maximum(top, pair[t, c, :MB])
        denom = jnp.zeros((MB, tile), jnp.float32)
        for c in range(n_camp):
            denom = denom + jnp.exp2(pair[t, c, :MB] - top) * pair[t, c, MB:]
        left = jnp.exp2(-top)
        denom = left + denom
        weight = jnp.exp2(mine - top) / denom
        if t == ROUNDS - 1:
            spare[...] = left / denom
        weight = jnp.transpose(jnp.concatenate([weight] * (tile // MB), axis=0))
        for k in range(MB):
            weight_of[k] = jnp.broadcast_to(weight[:, k : k + 1], (tile, tile))

        def uses(s, _):
            used = jnp.sum(exp_cost[s] * weight_of[rows[0, s]], axis=0, keepdims=True)
            picked[t, me, pl.ds(s, 1), :] = used
            return 0

        lax.fori_loop(0, slots, uses, 0, unroll=UNROLL)
        place = lax.broadcasted_iota(jnp.int32, (slots, tile), 0)
        picked[t, me] = jnp.where(place < count[0, 0], picked[t, me], 0.0)

        gather_start(picked.at[t], t + 1)
        gather_relay(picked.at[t], t + 1)
        if t == 0:
            for d in range(deep):
                gather_wait(ids, 0, d)
            mark()
        else:
            dense()
        for d in range(deep):
            gather_wait(picked.at[t], t + 1, d)
            rest = picked[t, pl.ds(level[d] * plane, plane)].reshape(plane * slots, tile)
            here = pl.ds(pl.multiple_of(level[d] * (plane * slots), 32), plane * slots)
            for i in range(3):
                part = rest.astype(jnp.bfloat16)
                parts[here, i * tile : (i + 1) * tile] = part
                rest = rest - part.astype(jnp.float32)

        if t < ROUNDS - 1:
            own_price[...] = advance(own_price[...], summed_by(own_hot[...]), own_allow[...])
        else:
            dense()

    gather_drain(ids, 0)
    for t in range(ROUNDS):
        gather_drain(picked.at[t], t + 1)
        for f in range(1, n_camp):
            camp_copy(t, f).wait_send()


def hand_over(price, usage, spare, price_out, usage_out, unused_out, sem):
    stores = [
        pltpu.make_async_copy(src, dst, sem.at[i])
        for i, (src, dst) in enumerate(
            ((price, price_out), (usage, usage_out), (spare, unused_out))
        )
    ]
    for store in stores:
        store.start()
    for store in stores:
        store.wait()


def local(n_mem, n_camp, gains, costs, tile_rows, tile_cols, tile_count, duals, allowances):
    slots, tile, _ = gains.shape
    blocks = duals.shape[0] // tile
    plane = 4 if n_mem % 4 == 0 else 1
    deep = n_mem // plane
    id_rows = -(-n_mem * slots // (8 * tile)) * 8
    f32, bf16 = jnp.float32, jnp.bfloat16
    anywhere = pl.BlockSpec(memory_space=pl.ANY)
    dma = pltpu.SemaphoreType.DMA
    shapes = ((blocks, tile), (blocks, tile), (MB, tile))
    held = pl.pallas_call(
        functools.partial(kernel, n_mem, n_camp, plane),
        out_shape=tuple(pltpu.VMEM(shape, f32) for shape in shapes),
        in_specs=[anywhere] * 7,
        out_specs=(pl.BlockSpec(memory_space=pltpu.VMEM),) * 3,
        scratch_shapes=[
            pltpu.VMEM((slots, tile, tile), bf16),
            pltpu.VMEM((slots, tile, tile), bf16),
            pltpu.VMEM((slots, tile, tile), f32),
            pltpu.VMEM((slots, tile, tile), f32),
            pltpu.VMEM((slots, tile, tile), f32),
            pltpu.VMEM((slots + 1, tile, tile), f32),
            pltpu.VMEM((slots, tile, tile), f32),
            pltpu.VMEM((MB, tile, tile), f32),
            pltpu.VMEM((MB, tile, tile), f32),
            pltpu.VMEM((ROUNDS, n_camp, 2 * MB, tile), f32),
            pltpu.VMEM((n_mem, id_rows, tile), jnp.int32),
            pltpu.VMEM((ROUNDS, n_mem, slots, tile), f32),
            pltpu.VMEM((blocks, n_mem * slots), bf16),
            pltpu.VMEM((slots, n_mem * slots), bf16),
            pltpu.VMEM((n_mem * slots, 3 * tile), bf16),
            pltpu.VMEM((blocks, tile), f32),
            pltpu.VMEM((slots, tile), jnp.int32),
            pltpu.VMEM((slots, tile), f32),
            pltpu.VMEM((slots, tile), f32),
            pltpu.SMEM((1, slots), jnp.int32),
            pltpu.SMEM((1, slots), jnp.int32),
            pltpu.SMEM((1, 1), jnp.int32),
            pltpu.SMEM((slots,), jnp.int32),
            pltpu.SMEM((MB,), jnp.int32),
            dma((7,)),
            dma((ROUNDS + 1, deep)),
            dma((ROUNDS + 1, deep)),
            dma((ROUNDS + 1, deep, plane)),
            dma((ROUNDS + 1, deep, plane)),
            dma((ROUNDS, n_camp)),
            dma((ROUNDS, n_camp)),
        ],
        compiler_params=pltpu.CompilerParams(
            collective_id=0, has_side_effects=True, vmem_limit_bytes=56 * 1024 * 1024
        ),
    )(
        gains, costs, tile_rows.T, tile_cols.T, tile_count,
        duals.reshape(blocks, tile), allowances.reshape(blocks, tile),
    )
    price, usage, unused = pl.pallas_call(
        hand_over,
        out_shape=tuple(jax.ShapeDtypeStruct(shape, f32) for shape in shapes),
        in_specs=[pl.BlockSpec(memory_space=pltpu.VMEM)] * 3,
        out_specs=(anywhere,) * 3,
        scratch_shapes=[dma((3,))],
        compiler_params=pltpu.CompilerParams(vmem_limit_bytes=1024 * 1024),
    )(*held)
    return price.reshape(-1), usage.reshape(-1), unused.reshape(-1)


def solution(mesh):
    return jax.shard_map(
        functools.partial(local, mesh.shape["mem"], mesh.shape["camp"]),
        mesh=mesh,
        in_specs=(
            P("mem", None, "camp"),
            P("mem", None, "camp"),
            P("mem", "camp"),
            P("mem", "camp"),
            P("mem", "camp"),
            P("camp"),
            P("camp"),
        ),
        out_specs=(P("camp"), P("camp"), P("mem")),
        check_vma=False,
    )
```
